256 devices in a mesh: gx: 16 (over z, core), gy: 16 (over x, y).
Axes of the slice: x: 4, y: 4, z: 8, core: 2. Of those that a mesh axis runs over, the one named last changes fastest.
Arguments:
- positions: float32 [16, 16, 3, 256], P('gx', 'gy'), may hold values from 0 to 10
- species: int32 [16, 16, 256], P('gx', 'gy'), may hold values from 0 to 5
- neighbours: int32 [16, 16, 256, 12], P('gx', 'gy'), may hold values from 0 to 2303
- counts: int32 [16, 16, 256], P('gx', 'gy'), may hold values from 6 to 12
- species_embed: float32 [6, 128], replicated, may hold values from -6 to 6
- radial: float32 [2, 2, 8, 128], replicated, may hold values from -2 to 2
- mixing: float32 [2, 2, 128, 128], replicated, may hold values from -0.5 to 0.5
- read_hidden: float32 [128, 128], replicated, may hold values from -0.5 to 0.5
- read_out: float32 [128], replicated, may hold values from -0.5 to 0.5
- charge_map: float32 [128, 64], replicated, may hold values from -0.5 to 0.5
- wavevectors: int32 [3, 4096], replicated, may hold values from -8 to 8, as said below
Outputs:
- forces: float32 [16, 16, 3, 256], P('gx', 'gy')
- site_energy: float32 [16, 16, 256], P('gx', 'gy')
The draws below stay inside these ranges and needn't reach their ends.
Inputs may be any that keep to these rules, and one draw needn't show every extreme that they name: `neighbours`: entry (3 a + b) * 256 + t names atom t of the cell offset by (a - 1, b - 1) along gx, gy, periodically. Slots n < counts are used. `wavevectors`: the 4096 triples are distinct, and no triple has its first two components both zero.
All inputs are finite; a program needn't handle non-finite values.
Results may differ from the reference program's by a relative error of at most 0.0017.
Values may be sent and summed in bfloat16 or wider, within the bound.
A program may use at most 128 MiB of HBM per device.

```python
import math
import jax
import jax.numpy as jnp
from jax import lax

ATOM_DEV = 256
NB = 12
C = 128
CL = 64
K = 4096
NR = 8
NS = 6
LAYERS = 2
N_GX = 16
N_GY = 16


def draw_wavevectors(key, part):
    order = jax.random.permutation(key, jnp.arange(4896, dtype=jnp.int32))[:K]
    pair_index = order // 17
    third = order % 17 - 8
    pair_index = pair_index + (pair_index >= 144).astype(jnp.int32)
    first = pair_index // 17 - 8
    second = pair_index % 17 - 8
    return jnp.stack([first, second, third]).astype(jnp.int32)


def touch_ends(values, key, least, largest):
    spot = [jax.random.randint(jax.random.fold_in(key, axis), (), 0, length) for axis, length in enumerate(values.shape)]
    widest = values.shape.index(max(values.shape))
    neighbour = spot[:widest] + [(spot[widest] + 1) % values.shape[widest]] + spot[widest + 1:]
    return values.at[tuple(spot)].set(least).at[tuple(neighbour)].set(largest)


def levels(stream_key, shape, pieces, smallest, top_value):
    def one(axis_at, parts):
        steps = jax.random.uniform(jax.random.fold_in(jax.random.fold_in(stream_key, 6), axis_at), (parts,), jnp.float32, smallest / len(pieces), top_value / len(pieces))
        return jnp.repeat(jnp.exp(steps), shape[axis_at] // parts).reshape((-1,) + (1,) * (len(shape) - axis_at - 1))

    level = one(*pieces[0])
    for cut in pieces[1:]:
        level = level * one(*cut)
    return level


def normal_values(rng, shape, width, most, kind=jnp.bfloat16):
    entries = jax.random.normal(rng, shape, jnp.float32) * width
    return jnp.minimum(jnp.maximum(entries, -most), most).astype(kind)


def setup_inputs(seed: int = 0) -> dict:
    key_list = jax.random.split(jax.random.key(seed), 12)
    return {
        "positions": jnp.clip(10.0 * jax.random.uniform(key_list[0], (N_GX, N_GY, 3, ATOM_DEV), jnp.float32) ** levels(key_list[0], (N_GX, N_GY, 3, ATOM_DEV), ((0, 16), (1, 16)), -0.2, 0.2), 0.0, 10.0),
        "species": touch_ends(jax.random.randint(key_list[1], (N_GX, N_GY, ATOM_DEV), 0, NS), jax.random.fold_in(key_list[1], 1), 0, NS - 1).astype(jnp.int32),
        "neighbours": touch_ends(jax.random.randint(key_list[2], (N_GX, N_GY, ATOM_DEV, NB), 0, 9 * ATOM_DEV), jax.random.fold_in(key_list[2], 1), 0, (9 * ATOM_DEV) - 1).astype(jnp.int32),
        "counts": touch_ends(jax.random.randint(key_list[3], (N_GX, N_GY, ATOM_DEV), NB // 2, NB + 1), jax.random.fold_in(key_list[3], 1), NB // 2, NB).astype(jnp.int32),
        "species_embed": normal_values(key_list[4], (NS, C), 1.0, 6.0, jnp.float32),
        "radial": normal_values(key_list[5], (LAYERS, 2, NR, C), NR ** -0.5, 2.0, jnp.float32),
        "mixing": normal_values(key_list[6], (LAYERS, 2, C, C), C ** -0.5, 0.5, jnp.float32),
        "read_hidden": normal_values(key_list[7], (C, C), C ** -0.5, 0.5, jnp.float32),
        "read_out": normal_values(key_list[8], (C,), C ** -0.5, 0.5, jnp.float32),
        "charge_map": normal_values(key_list[9], (C, CL), C ** -0.5, 0.5, jnp.float32),
        "wavevectors": draw_wavevectors(jax.random.fold_in(key_list[11], 71), 0),
    }


cell_width = 10.0
box_height = 30.0
cut_radius = 50.0
soften = 0.25
screen = 0.5
smear_width = 0.5
highest = lax.Precision.HIGHEST

def build_frame(extended):
    offsets = (jnp.arange(3, dtype=jnp.float32) - 1.0) * cell_width
    shift_x = jnp.broadcast_to(offsets[:, None], (3, 3))
    shift_y = jnp.broadcast_to(offsets[None, :], (3, 3))
    shifts = jnp.stack([shift_x, shift_y, jnp.zeros((3, 3), jnp.float32)], axis=2)
    coords = extended[:, :, :3, :] + shifts[:, :, :, None]
    src_pos = jnp.moveaxis(coords, 2, 0).reshape(3, -1)
    kind_codes = extended[:, :, 3, :].reshape(-1)
    return (src_pos, kind_codes)

def embed_rows(kind_codes, species_embed):
    lookup = (kind_codes[:, None] == jnp.arange(species_embed.shape[0], dtype=jnp.float32)[None, :]).astype(jnp.float32)
    return jnp.dot(lookup, species_embed, precision=highest)

def interact(h_dst, h_src, own_pos, src_pos, neighbour_ids, slot_counts, radial_pair, mix_pair):
    slots = neighbour_ids.shape[1]
    orders = radial_pair.shape[1]
    relative = src_pos[:, neighbour_ids] - own_pos[:, :, None]
    distance = jnp.sqrt(lax.optimization_barrier(jnp.sum(relative * relative, axis=0)) + soften)
    unit_vec = relative / distance[None]
    frequency = jnp.arange(1, orders + 1, dtype=jnp.float32) * (math.pi / cut_radius)
    arg_scaled = distance[:, :, None] * frequency
    radial_basis = jnp.sin(arg_scaled) / arg_scaled
    live_slots = (jnp.arange(slots)[None, :] < slot_counts[:, None]).astype(jnp.float32)
    weight_zero = jnp.einsum('anr,rc->anc', radial_basis, radial_pair[0], precision=highest) * live_slots[:, :, None]
    weight_one = jnp.einsum('anr,rc->anc', radial_basis, radial_pair[1], precision=highest) * live_slots[:, :, None]
    source = h_src[neighbour_ids]
    norm_factor = 1.0 / math.sqrt(slots)
    msg_zero = lax.optimization_barrier(jnp.sum(weight_zero * source, axis=1)) * norm_factor
    msg_one = jnp.einsum('anc,xan->xac', weight_one * source, unit_vec, precision=highest) * norm_factor
    squares = lax.optimization_barrier(jnp.sum(msg_one * msg_one, axis=0))
    preact = jnp.dot(msg_zero, mix_pair[0], precision=highest) + jnp.dot(squares, mix_pair[1], precision=highest)
    return h_dst + jax.nn.silu(preact)

def first_layer(own_pos, src_pos, initial_src, neighbour_ids, slot_counts, radial, mixing):
    atom_count = own_pos.shape[1]
    return interact(initial_src[4 * atom_count:5 * atom_count], initial_src, own_pos, src_pos, neighbour_ids, slot_counts, radial[0], mixing[0])

def second_section(hidden_src, own_pos, src_pos, neighbour_ids, slot_counts, radial, mixing, read_hidden, read_out, charge_map):
    atom_count = own_pos.shape[1]
    hidden_two = interact(hidden_src[4 * atom_count:5 * atom_count], hidden_src, own_pos, src_pos, neighbour_ids, slot_counts, radial[1], mixing[1])
    energy = jnp.dot(jax.nn.silu(jnp.dot(hidden_two, read_hidden, precision=highest)), read_out, precision=highest)
    charges = jnp.dot(hidden_two, charge_map, precision=highest)
    return (energy, charges)

def wave_terms(wavevectors, grid_x, grid_y):
    lengths = jnp.array([grid_x * cell_width, grid_y * cell_width, box_height], dtype=jnp.float32)
    wave_phys = 2.0 * math.pi * wavevectors.astype(jnp.float32) / lengths[:, None]
    wave_sq = lax.optimization_barrier(jnp.sum(wave_phys * wave_phys, axis=0))
    green_weight = jnp.exp(-smear_width * wave_sq) / (wave_sq + screen * screen)
    return (wave_phys, green_weight)

def phase_pair(global_pos, wave_part):
    angle = global_pos[0][:, None] * wave_part[0][None, :] + global_pos[1][:, None] * wave_part[1][None, :] + global_pos[2][:, None] * wave_part[2][None, :]
    return (jnp.cos(angle), jnp.sin(angle))

def structure_term(charges, global_pos, wave_part):
    cosine, sine_part = phase_pair(global_pos, wave_part)
    dims = (((0,), (0,)), ((), ()))
    real_part = lax.dot_general(cosine, charges, dims, precision=highest)
    imag_part = lax.dot_general(sine_part, charges, dims, precision=highest)
    return jnp.concatenate([real_part, imag_part], axis=1)

def fold_terms(carried, piece_rows, start_row, charges, global_pos, wave_phys):
    potential, lr_grad = carried
    row_count = piece_rows.shape[0]
    lat_width = charges.shape[1]
    wave_part = lax.dynamic_slice_in_dim(wave_phys, jnp.asarray(start_row).astype(jnp.int32), row_count, 1)
    cosine, sine_part = phase_pair(global_pos, wave_part)
    weight_re = piece_rows[:, :lat_width]
    weight_im = piece_rows[:, lat_width:]
    potential = potential + jnp.dot(cosine, weight_re, precision=highest) + jnp.dot(sine_part, weight_im, precision=highest)
    dims = (((1,), (1,)), ((), ()))
    proj_re = lax.dot_general(charges, weight_re, dims, precision=highest)
    proj_im = lax.dot_general(charges, weight_im, dims, precision=highest)
    phase_turn = cosine * proj_im - sine_part * proj_re
    lr_grad = lr_grad + lax.dot_general(wave_part, phase_turn, dims, precision=highest)
    return (potential, lr_grad)

def reference(positions, species, neighbours, counts, species_embed, radial, mixing, read_hidden, read_out, charge_map, wavevectors):
    grid_x = positions.shape[0]
    grid_y = positions.shape[1]
    atom_count = positions.shape[3]
    device_total = grid_x * grid_y
    lat_width = charge_map.shape[1]
    wave_count = wavevectors.shape[1]
    kind_all = species.astype(jnp.float32)[:, :, None, :]

    def neighbour_block(lookup, device):
        row_index = device // grid_y
        col_index = device % grid_y
        row_ids = (row_index + jnp.arange(3) - 1) % grid_x
        col_ids = (col_index + jnp.arange(3) - 1) % grid_y
        return (lookup[row_ids[:, None], col_ids[None, :]], row_index, col_index)

    def layer_one_all(pos_all):
        packed = jnp.concatenate([pos_all, kind_all], axis=2)

        def single(device):
            extended, row_index, col_index = neighbour_block(packed, device)
            src_pos, kind_codes = build_frame(extended)
            initial_src = embed_rows(kind_codes, species_embed)
            return first_layer(pos_all[row_index, col_index], src_pos, initial_src, neighbours[row_index, col_index], counts[row_index, col_index], radial, mixing)
        result = lax.map(jax.checkpoint(single), jnp.arange(device_total))
        return result.reshape(grid_x, grid_y, atom_count, -1)
    hidden_one, pull_one = jax.vjp(layer_one_all, positions)
    hidden_low = lax.optimization_barrier(hidden_one.astype(jnp.bfloat16)).astype(jnp.float32)

    def section_two_all(hidden_all, pos_all):
        packed = jnp.concatenate([pos_all, kind_all], axis=2)

        def single(device):
            extended, row_index, col_index = neighbour_block(packed, device)
            src_pos, kind_codes = build_frame(extended)
            hidden_ext, row_same, col_same = neighbour_block(hidden_all, device)
            hidden_src = hidden_ext.reshape(9 * atom_count, -1)
            return second_section(hidden_src, pos_all[row_index, col_index], src_pos, neighbours[row_index, col_index], counts[row_index, col_index], radial, mixing, read_hidden, read_out, charge_map)
        return lax.map(jax.checkpoint(single), jnp.arange(device_total))
    (energy_sr, charges), pull_two = jax.vjp(section_two_all, hidden_low, positions)
    wave_phys, green_weight = wave_terms(wavevectors, grid_x, grid_y)
    device_ids = jnp.arange(device_total)
    anchor = jnp.stack([(device_ids // grid_y).astype(jnp.float32) * cell_width, (device_ids % grid_y).astype(jnp.float32) * cell_width, jnp.zeros((device_total,), jnp.float32)], axis=1)
    global_all = positions.reshape(device_total, 3, atom_count) + anchor[:, :, None]

    def add_term(running, members):
        return (running + structure_term(members[0], members[1], wave_phys), None)
    structure, unused = lax.scan(add_term, jnp.zeros((wave_count, 2 * lat_width), jnp.float32), (charges, global_all))
    weighted = green_weight[:, None] * structure

    def per_device(members):
        start_state = (jnp.zeros((atom_count, lat_width), jnp.float32), jnp.zeros((3, atom_count), jnp.float32))
        return fold_terms(start_state, weighted, 0, members[0], members[1], wave_phys)
    potential, lr_grad = lax.map(per_device, (charges, global_all))
    lr_scale = 1.0 / math.sqrt(wave_count * lat_width * device_total * atom_count)
    site_energy = energy_sr + lr_scale * lax.optimization_barrier(jnp.sum(charges * potential, axis=2))
    grad_hidden, grad_pos_two = pull_two((jnp.ones_like(energy_sr), 2.0 * lr_scale * potential))
    grad_pos_one = pull_one(grad_hidden)[0]
    forces = -(grad_pos_one + grad_pos_two + 2.0 * lr_scale * lr_grad.reshape(grid_x, grid_y, 3, atom_count))
    return (forces, site_energy.reshape(grid_x, grid_y, atom_count))
```

```python
import functools
import math

import jax
import jax.numpy as jnp
from jax import lax
from jax.experimental import pallas as pl
from jax.experimental.pallas import tpu as pltpu
from jax.sharding import PartitionSpec as P

MESH = pl.DeviceIdType.MESH
f32, bf16 = jnp.float32, jnp.bfloat16
NN, NT, TN = ((1,), (0,)), ((1,), (1,)), ((0,), (0,))
CELL, HEIGHT, CUT = 10.0, 30.0, 50.0
AT, NB, C, NR, NS = 256, 12, 128, 8, 6
E = AT * NB
HALF = 1280
KZ = 9
LANES = 384
NORM = 1.0 / math.sqrt(NB)


def dot(a, b, dims):
    return lax.dot_general(a, b, (dims, ((), ())), preferred_element_type=f32)


def split2(x):
    hi = x.astype(bf16)
    return hi, (x - hi.astype(f32)).astype(bf16)


def split3(x):
    hi = x.astype(bf16)
    rest = x - hi.astype(f32)
    mid = rest.astype(bf16)
    return hi, mid, (rest - mid.astype(f32)).astype(bf16)


def dot3(a, b, dims):
    ah, al = split2(a)
    bh, bl = split2(b)
    return dot(ah, bh, dims) + dot(ah, bl, dims) + dot(al, bh, dims)


def rowid(shape):
    return lax.broadcasted_iota(jnp.int32, shape, 0)


def laneid(shape):
    return lax.broadcasted_iota(jnp.int32, shape, 1)


def sigmoid(x):
    return 1.0 / (1.0 + jnp.exp(-x))


def silu_pair(x):
    s = sigmoid(x)
    return x * s, s * (1.0 + x * (1.0 - s))


def swap_rows(x):
    h = x.shape[0] // 2
    return jnp.concatenate([x[h:], x[:h]], axis=0)


def swap_lanes(x):
    h = x.shape[1] // 2
    return jnp.concatenate([x[:, h:], x[:, :h]], axis=1)


def colsum(x):
    return jnp.sum(x, axis=0, keepdims=True)


def one_hot(idx_row):
    f = jnp.where(idx_row >= HALF, idx_row - HALF, idx_row)
    return jnp.where(rowid((HALF, AT)) == f, 1.0, 0.0).astype(bf16)


def pos_table(frame):
    cells = []
    for s in range(9):
        a, b = divmod(s, 3)
        r = rowid((8, AT))
        shift = jnp.where(r == 0, CELL * (a - 1), 0.0) + jnp.where(r == 1, CELL * (b - 1), 0.0)
        cells.append(frame[s] + shift)
    cells.append(jnp.zeros((8, AT), f32))
    parts = []
    for half in (cells[:5], cells[5:]):
        parts += [t.astype(f32) for t in split3(jnp.concatenate(half, axis=1))]
    return jnp.concatenate(parts, axis=0).astype(bf16)


def geometry(gathered, idx, own, cnt):
    low = gathered[0:8] + gathered[8:16] + gathered[16:24]
    high = gathered[24:32] + gathered[32:40] + gathered[40:48]
    pos = jnp.where(idx >= HALF, high, low)
    rel = jnp.where(rowid((8, E)) < 3, pos - jnp.concatenate([own] * NB, axis=1), 0.0)
    kind = pos[3:4]
    dist = jnp.sqrt(colsum(rel * rel) + 0.25)
    inv = 1.0 / dist
    unit = rel * inv
    freq = (rowid((8, 1)) + 1).astype(f32) * (math.pi / CUT)
    arg = dist * freq
    live = jnp.concatenate([jnp.where(n < cnt, 1.0, 0.0) for n in range(NB)], axis=1)
    basis = jnp.sin(arg) / arg
    slope = (jnp.cos(arg) - basis) * (inv * live)
    return basis * live, slope, unit, inv, kind


def chain(db, du, slope, unit, inv):
    return du * inv + unit * (colsum(db * slope) - inv * colsum(du * unit))


def kind_rows(kind):
    return jnp.where(rowid((8, AT)).astype(f32) == kind, 1.0, 0.0).astype(bf16)


def embed_cols(embed8, kind):
    oh = kind_rows(kind)
    hi, mid, lo = split3(embed8)
    return dot(hi, oh, TN) + dot(mid, oh, TN) + dot(lo, oh, TN)


def first_sums(basis, unit, kind):
    sums = [jnp.zeros((32, AT), f32) for _ in range(NS)]
    for n in range(NB):
        sl = slice(n * AT, (n + 1) * AT)
        b, u, k = basis[:, sl], unit[:, sl], kind[:, sl]
        z = jnp.concatenate([b, b * u[0:1], b * u[1:2], b * u[2:3]], axis=0)
        for s in range(NS):
            sums[s] = sums[s] + jnp.where(k == float(s), z, 0.0)
    return [jnp.concatenate([t[8 * p : 8 * p + 8] for t in sums], axis=0) for p in range(4)]


def pair_rows(radial, embed8):
    return jnp.concatenate([radial * embed8[s : s + 1] for s in range(NS)], axis=0)


def layer_one(sums, own_kind, radial0, radial1, mix0, mix1, embed8):
    re0, re1 = pair_rows(radial0, embed8), pair_rows(radial1, embed8)
    m0 = dot3(re0, sums[0], TN) * NORM
    m1 = dot3(re1, jnp.concatenate(sums[1:], axis=1), TN) * NORM
    mx = [m1[:, p * AT : (p + 1) * AT] for p in range(3)]
    sq = mx[0] * mx[0] + mx[1] * mx[1] + mx[2] * mx[2]
    act, slope = silu_pair(dot3(mix0, m0, TN) + dot3(mix1, sq, TN))
    return embed_cols(embed8, own_kind) + act, slope, m1


def layer_one_back(grad, slope, m1, radial0, radial1, mix0, mix1, embed8):
    re0, re1 = pair_rows(radial0, embed8), pair_rows(radial1, embed8)
    dpre = grad * slope
    d0 = dot3(mix0, dpre, NN) * NORM
    dsq = dot3(mix1, dpre, NN) * (2.0 * NORM)
    d1 = m1 * jnp.concatenate([dsq] * 3, axis=1)
    a0 = dot3(re0, d0, NN)
    a1 = dot3(re1, d1, NN)
    return [a0] + [a1[:, p * AT : (p + 1) * AT] for p in range(3)]


def first_sums_back(n, sums, basis, unit, kind):
    z = []
    for t in sums:
        got = jnp.zeros((8, AT), f32)
        for s in range(NS):
            got = jnp.where(kind == float(s), t[8 * s : 8 * s + 8], got)
        z.append(got)
    db = z[0] + z[1] * unit[0:1] + z[2] * unit[1:2] + z[3] * unit[2:3]
    du = [colsum(basis * t) for t in z[1:]]
    return db, jnp.concatenate(du + [jnp.zeros((5, AT), f32)], axis=0)


def radial_left(radial0, radial1):
    r = jnp.concatenate([radial0, radial1], axis=1)
    hi, lo = split2(r)
    hi, lo = hi.astype(f32), lo.astype(f32)
    return jnp.concatenate([hi, hi, lo, jnp.zeros_like(hi)], axis=0).T.astype(bf16)


def basis_right(b):
    hi, lo = split2(b)
    hi, lo = hi.astype(f32), lo.astype(f32)
    return jnp.concatenate([hi, lo, hi, jnp.zeros_like(hi)], axis=0).astype(bf16)


def second_slot(folded, oh, idx_row, left, b):
    both = dot(folded, oh, NN)
    g = jnp.where(idx_row >= HALF, both[C:], both[:C])
    return g, dot(left, basis_right(b), NN)


def second_slot_back(g, w, idx_row, unit, d0, d1, rhi, rstack):
    w0, w1 = w[:C], w[C:]
    ux, uy, uz = unit[0:1], unit[1:2], unit[2:3]
    p = d1[0] * ux + d1[1] * uy + d1[2] * uz
    dg = w0 * d0 + w1 * p
    xh, xl = split2(jnp.concatenate([g * d0, g * p], axis=0))
    both = dot(rstack, xh, NN)
    db = both[:8] + both[8:] + dot(rhi, xl, NN)
    t = w1 * g
    du = [colsum(t * d) for d in d1]
    du = jnp.concatenate(du + [jnp.zeros((5, AT), f32)], axis=0)
    far = idx_row >= HALF
    dgm = jnp.concatenate([jnp.where(far, 0.0, dg), jnp.where(far, dg, 0.0)], axis=0)
    return dgm, db, du


def trig8(pos_row, origin, length):
    theta = (pos_row + origin) * (2.0 * math.pi / length)
    arg = theta * (rowid((8, 1)) + 1).astype(f32)
    return jnp.cos(arg), jnp.sin(arg)


def phases(pos, ox, oy, lx, ly, cq):
    c1, s1 = trig8(pos[0:1], ox, lx)
    c2, s2 = trig8(pos[1:2], oy, ly)
    c3, s3 = trig8(pos[2:3], 0.0, HEIGHT)
    cos, sin = [], []
    for m in range(8):
        a, b = c1[m : m + 1], s1[m : m + 1]
        cc, ss, sc, cs = a * c2, b * s2, b * c2, a * s2
        cos += [cc - ss, cc + ss]
        sin += [sc + cs, sc - cs]
    gap = [jnp.zeros((48, AT), f32)]
    plane = jnp.concatenate(cos + sin + [c1, c2] + gap + [s1, s2] + gap, axis=0)
    third = [jnp.where(rowid((2 * cq, AT)) < cq, 1.0, 0.0)]
    for m in range(8):
        third.append(jnp.where(rowid((2 * cq, AT)) < cq, c3[m : m + 1], s3[m : m + 1]))
    return plane, jnp.concatenate(third, axis=0)


def wave_cols(waves):
    k1, k2, k3 = waves[0:1], waves[1:2], waves[2:3]
    flip = (k1 < 0) | ((k1 == 0) & (k2 < 0))
    k1, k2, k3 = (jnp.where(flip, -k, k) for k in (k1, k2, k3))
    main = (k1 - 1) * 16 + jnp.where(k2 > 0, k2 - 1, 7 - k2)
    col = jnp.where(k1 == 0, 135 + k2, jnp.where(k2 == 0, 127 + k1, main))
    return col, k3


def count_part(col, k3, kappa):
    oh = jnp.where(rowid((256, AT)) == col, 1.0, 0.0).astype(bf16)
    r = rowid((8, AT))
    want = jnp.where(r == 0, kappa, jnp.where(r == 1, -kappa, 99))
    return dot(jnp.where(k3 == want, 1.0, 0.0).astype(bf16), oh, NT)


def col_numbers():
    lane = laneid((1, 256))
    low = (lane & 7) + 1
    k1 = jnp.where(lane < 128, (lane >> 4) + 1, jnp.where(lane < 136, low, 0))
    k2 = jnp.where(lane < 128, jnp.where((lane & 15) < 8, low, -low), jnp.where(lane < 136, 0, low))
    k2 = jnp.where(lane < 144, k2, 0)
    return k1.astype(f32), k2.astype(f32)


def widen(x):
    main, rest = x[:, :128], x[:, 128:]
    rest = jnp.where(laneid(rest.shape) < 64, rest, swap_lanes(rest))
    return jnp.concatenate([main, main, rest], axis=1)


def weights(count, kappa, lx, ly):
    k1, k2 = col_numbers()
    kz = kappa.astype(f32)
    wx, wy, wz = 2.0 * math.pi * k1 / lx, 2.0 * math.pi * k2 / ly, 2.0 * math.pi * kz / HEIGHT
    sq = wx * wx + wy * wy + wz * wz
    green = jnp.exp(-0.5 * sq) / (sq + 0.25)
    plus = count[0:1] * green
    minus = jnp.where(kappa == 0, 0.0, count[1:2] * green)
    return widen(plus + minus), widen(plus - minus)


def turn(t, sign):
    rest = t[:, 256:]
    swapped = swap_lanes(rest)
    rest = jnp.where(laneid(rest.shape) < 64, sign * swapped, -sign * swapped)
    return jnp.concatenate([sign * t[:, 128:256], -sign * t[:, :128], rest], axis=1)


def weigh(t, sigma, delta):
    cq = t.shape[0] // 2
    sign = jnp.where(rowid((2 * cq, 1)) < cq, -1.0, 1.0)
    return sigma * t + delta * turn(swap_rows(t), sign)


def fold_left(v, lx, ly):
    k1, k2 = col_numbers()
    kx, ky = widen(k1) * (2.0 * math.pi / lx), widen(k2) * (2.0 * math.pi / ly)
    t = turn(v, 1.0)
    return jnp.concatenate([v, kx * t, ky * t], axis=0)


def fold_cell(u, third, q):
    cq = q.shape[0]
    rows = KZ * 2 * cq
    zero = jnp.zeros((2 * cq, AT), f32)
    pot, gx, gy, gz = zero, zero, zero, zero
    for k in range(KZ):
        at = slice(k * 2 * cq, (k + 1) * 2 * cq)
        t, part = third[at], u[at]
        pot = pot + t * part
        gx = gx + t * u[rows:][at]
        gy = gy + t * u[2 * rows :][at]
        if k:
            gz = gz + swap_rows(t) * (part * (2.0 * math.pi * k / HEIGHT))
    qq = jnp.concatenate([q, q], axis=0)
    sign = jnp.where(rowid((2 * cq, 1)) < cq, -1.0, 1.0)
    rows = [pot[:cq] + pot[cq:], colsum(qq * gx), colsum(qq * gy), colsum(qq * gz * sign)]
    return jnp.concatenate(rows + [jnp.zeros((1, AT), f32)], axis=0)


def kernel(
    gx_n,
    gy_n,
    pos_ref,
    kind_ref,
    nbr_ref,
    cnt_ref,
    emb_ref,
    rad_ref,
    mix_ref,
    rh_ref,
    ro_ref,
    cm_ref,
    wave_ref,
    force_ref,
    site_ref,
    pfr,
    prow,
    hfr,
    oht,
    gfold,
    g_s,
    w_s,
    dgm_s,
    drel_s,
    basis_s,
    slope_s,
    unit_s,
    misc_s,
    m_s,
    ah,
    al,
    tr,
    t_s,
    q_send,
    q_recv,
    t_send,
    t_recv,
    v_send,
    v_all,
    b_send,
    b_recv,
    g_send,
    g_recv,
    f_send,
    f_recv,
    halo_s,
    halo_r,
    row_s,
    row_r,
    red_s,
    red_r,
    bc_s,
    bc_r,
):
    mx, my = lax.axis_index("gx"), lax.axis_index("gy")
    cq = cm_ref.shape[1] // gx_n
    lx, ly = CELL * gx_n, CELL * gy_n
    atoms_all = AT * gx_n * gy_n
    scale = 1.0 / math.sqrt(wave_ref.shape[1] * cm_ref.shape[1] * atoms_all)

    def cell(da, db):
        return lax.rem(mx + da + gx_n, gx_n), lax.rem(my + db + gy_n, gy_n)

    around = [(da, db) for da in (-1, 0, 1) for db in (-1, 0, 1) if (da, db) != (0, 0)]

    def remote(src, dst, ssem, rsem, dev):
        return pltpu.make_async_remote_copy(
            src_ref=src,
            dst_ref=dst,
            send_sem=ssem,
            recv_sem=rsem,
            device_id=dev,
            device_id_type=MESH,
        )

    def halo(stage, src_of, dst):
        copies = []
        for da, db in around:
            here, there = 3 * (da + 1) + db + 1, 3 * (1 - da) + 1 - db
            copies.append(
                remote(
                    src_of(here),
                    dst.at[there],
                    halo_s.at[stage, here],
                    halo_r.at[stage, there],
                    cell(da, db),
                )
            )
            copies[-1].start()
        return copies

    pending = []

    barrier = pltpu.get_barrier_semaphore()
    mates = [cell(d, 0) for d in range(1, gx_n)] + [cell(0, d) for d in range(1, gy_n)]
    mates += [cell(da, db) for da, db in around if da and db]
    for dev in mates:
        pl.semaphore_signal(barrier, inc=1, device_id=dev, device_id_type=MESH)

    row = rowid((8, AT))
    own = jnp.where(row == 3, kind_ref[0].astype(f32), 0.0)
    for p in range(3):
        own = jnp.where(row == p, pos_ref[0, 0, p : p + 1, :], own)
    pfr[4] = own
    prow[0] = own
    pl.semaphore_wait(barrier, len(mates))

    copies = halo(0, lambda here: pfr.at[4], pfr)
    row_pos = [
        remote(prow.at[0], prow.at[d], row_s.at[0, d], row_r.at[0, d], cell(d, 0))
        for d in range(1, gx_n)
    ]
    for c in row_pos:
        c.start()
    pending += copies + row_pos

    def slot(n):
        return pl.ds(pl.multiple_of(n * AT, AT), AT)

    def hot(n, _):
        oht[:, slot(n)] = one_hot(nbr_ref[pl.ds(n, 1), :])
        return 0

    lax.fori_loop(0, NB, hot, 0)
    embed8 = jnp.zeros((8, C), f32)
    for s in range(NS):
        embed8 = jnp.where(rowid((8, C)) == s, emb_ref[s : s + 1, :], embed8)
    idx = jnp.concatenate([nbr_ref[n : n + 1, :] for n in range(NB)], axis=1)
    for c in copies:
        c.wait_recv()

    gathered = dot(pos_table([pfr[s] for s in range(9)]), oht[...], NN)
    basis, slope, unit, inv, kind = geometry(gathered, idx, own, cnt_ref[0])
    basis_s[...] = basis
    slope_s[...] = slope
    unit_s[...] = unit
    misc_s[0:1] = inv
    misc_s[1:2] = kind
    layer = (rad_ref[0, 0], rad_ref[0, 1], mix_ref[0, 0], mix_ref[0, 1], embed8)
    hidden, slope1, m1_first = layer_one(first_sums(basis, unit, kind), own[3:4], *layer)
    hfr[4] = hidden.astype(bf16)
    copies = halo(1, lambda here: hfr.at[4], hfr)
    pending += copies

    for c in row_pos:
        c.wait_recv()

    def phase(d, _):
        source = lax.rem(mx - d + gx_n, gx_n)
        plane, third = phases(
            prow[d], source.astype(f32) * CELL, my.astype(f32) * CELL, lx, ly, cq
        )
        hi, lo = split2(plane)
        ah[d] = hi
        al[d] = lo
        tr[d] = third
        return 0

    lax.fori_loop(0, gx_n, phase, 0)
    owners = [k * gy_n // KZ for k in range(KZ)]
    kappa = (my * KZ + gy_n - 1) // gy_n
    owning = (kappa < KZ) & ((kappa * gy_n) // KZ == my)
    kappa = jnp.minimum(kappa, KZ - 1)

    def count(s, total):
        col, k3 = wave_cols(wave_ref[:, slot(s)])
        return total + count_part(col, k3, kappa)

    counted = lax.fori_loop(0, wave_ref.shape[1] // AT, count, jnp.zeros((8, AT), f32))
    sigma, delta = weights(counted, kappa, lx, ly)
    left = radial_left(rad_ref[1, 0], rad_ref[1, 1])
    for c in copies:
        c.wait_recv()

    for s in range(9):
        part = slice(0, C) if s < 5 else slice(C, 2 * C)
        gfold[part, (s % 5) * AT : (s % 5 + 1) * AT] = hfr[s]
    gfold[C:, 4 * AT :] = jnp.zeros((C, AT), bf16)
    m_s[...] = jnp.zeros_like(m_s)

    def forward(n, _):
        g, w = second_slot(
            gfold[...], oht[:, slot(n)], nbr_ref[pl.ds(n, 1), :], left, basis_s[:, slot(n)]
        )
        g_s[n] = g.astype(bf16)
        w_s[n] = w
        u = unit_s[:, slot(n)]
        m_s[0] += w[:C] * g
        t = w[C:] * g
        for p in range(3):
            m_s[1 + p] += t * u[p : p + 1]
        return 0

    lax.fori_loop(0, NB, forward, 0)
    m1 = [m_s[1 + p] * NORM for p in range(3)]
    sq = m1[0] * m1[0] + m1[1] * m1[1] + m1[2] * m1[2]
    act, slope2 = silu_pair(
        dot3(mix_ref[1, 0], m_s[0] * NORM, TN) + dot3(mix_ref[1, 1], sq, TN)
    )
    h2 = hfr[4].astype(f32) + act
    q = dot3(cm_ref[...], h2, TN)
    for p in range(gx_n):
        q_send[p] = jnp.concatenate([q[cq * p : cq * p + cq]] * 2, axis=0)
    q_recv[0] = q_send[mx]
    copies = []
    for d in range(1, gx_n):
        dev = cell(d, 0)
        copies.append(
            remote(q_send.at[dev[0]], q_recv.at[d], row_s.at[1, d], row_r.at[1, d], dev)
        )
        copies[-1].start()
    pending += copies
    r, rs = silu_pair(dot3(rh_ref[...], h2, TN))
    ro8 = jnp.broadcast_to(ro_ref[...], (8, C))
    energy = dot3(ro8, r, NN)[0:1]
    dread = dot3(rh_ref[...] * ro_ref[...], rs, NN)
    for c in copies:
        c.wait_recv()

    t_s[...] = jnp.zeros_like(t_s)

    def gather_terms(d, _):
        qh, ql = split2(tr[d] * jnp.concatenate([q_recv[d]] * KZ, axis=0))
        t_s[...] += dot(qh, ah[d], NT) + dot(ql, ah[d], NT) + dot(qh, al[d], NT)
        return 0

    lax.fori_loop(0, gx_n, gather_terms, 0)
    rows = 2 * cq
    for k in range(KZ):
        t_send[k] = t_s[k * rows : (k + 1) * rows, :]
    to_owner = []
    for k in range(KZ):
        to_owner.append(
            remote(t_send.at[k], t_recv.at[my], red_s.at[k], red_r.at[my], (mx, owners[k]))
        )
        pl.when(my != owners[k])(to_owner[-1].start)

    spread = [
        remote(v_send, v_all.at[kappa], bc_s.at[d], bc_r.at[kappa], cell(0, d))
        for d in range(1, gy_n)
    ]

    @pl.when(owning)
    def _():
        t_recv[my] = t_send[kappa]
        for d in range(1, gy_n):
            src = lax.rem(my + d, gy_n)
            remote(
                t_send.at[0], t_recv.at[src], red_s.at[0], red_r.at[src], (mx, src)
            ).wait_recv()
        total = t_recv[0]
        for j in range(1, gy_n):
            total = total + t_recv[j]
        v = weigh(total, sigma, delta)
        v_send[...] = v
        v_all[kappa] = v
        for c in spread:
            c.start()

    for k in range(KZ):
        arrive = remote(v_send, v_all.at[k], bc_s.at[0], bc_r.at[k], (mx, owners[k]))
        pl.when(my != owners[k])(arrive.wait_recv)

    lh, ll = split2(
        fold_left(jnp.concatenate([v_all[k] for k in range(KZ)], axis=0), lx, ly)
    )

    def back(d):
        dev = cell(-d, 0)
        return remote(b_send.at[d], b_recv.at[mx], row_s.at[2, d], row_r.at[2, d], dev)

    def fold(step, _):
        d = lax.rem(step, gx_n)
        u = dot(lh, ah[d], NN) + dot(ll, ah[d], NN) + dot(lh, al[d], NN)
        b_send[d] = fold_cell(u, tr[d], q_recv[d, :cq])

        @pl.when(d > 0)
        def _():
            back(d).start()

        return 0

    lax.fori_loop(1, gx_n + 1, fold, 0)
    b_recv[mx] = b_send[0]
    for d in range(1, gx_n):
        src = lax.rem(mx + d, gx_n)
        remote(
            b_send.at[d], b_recv.at[src], row_s.at[2, d], row_r.at[2, d], (src, my)
        ).wait_recv()
    pot = jnp.concatenate([b_recv[p, :cq] for p in range(gx_n)], axis=0)
    long_range = b_recv[0]
    for p in range(1, gx_n):
        long_range = long_range + b_recv[p]
    site_ref[0] = energy + scale * colsum(q * pot)

    dh = dread + dot3(cm_ref[...], pot * (2.0 * scale), NN)
    dpre = dh * slope2
    d0 = dot3(mix_ref[1, 0], dpre, NN) * NORM
    dsq = dot3(mix_ref[1, 1], dpre, NN) * (2.0 * NORM)
    m_s[0] = d0
    for p in range(3):
        m_s[1 + p] = m1[p] * dsq
    rhi, rlo = split2(jnp.concatenate([rad_ref[1, 0], rad_ref[1, 1]], axis=1))
    rstack = jnp.concatenate([rhi.astype(f32), rlo.astype(f32)], axis=0).astype(bf16)

    def backward(n, _):
        u = unit_s[:, slot(n)]
        dgm, db, du = second_slot_back(
            g_s[n].astype(f32),
            w_s[n],
            nbr_ref[pl.ds(n, 1), :],
            u,
            m_s[0],
            [m_s[1], m_s[2], m_s[3]],
            rhi,
            rstack,
        )
        dgm_s[:, slot(n)] = dgm.astype(bf16)
        drel_s[:, slot(n)] = chain(db, du, slope_s[:, slot(n)], u, misc_s[0:1, slot(n)])
        return 0

    lax.fori_loop(0, NB, backward, 0)
    cells = dot(dgm_s[...], oht[...], NT)
    for s in range(9):
        part = cells[:C] if s < 5 else cells[C:]
        g_send[s] = part[:, (s % 5) * AT : (s % 5 + 1) * AT].astype(bf16)
    copies = halo(2, lambda here: g_send.at[here], g_recv)
    pending += copies
    grad = dh + cells[:C, 4 * AT :]
    for c in copies:
        c.wait_recv()
    for s in range(9):
        if s != 4:
            grad = grad + g_recv[s].astype(f32)

    sums = layer_one_back(grad, slope1, m1_first, *layer)
    own_grad = jnp.zeros((8, AT), f32)
    drels = []
    for n in range(NB):
        sl = slice(n * AT, (n + 1) * AT)
        b, u = basis_s[:, sl], unit_s[:, sl]
        db, du = first_sums_back(n, sums, b, u, misc_s[1:2, sl])
        drel = drel_s[:, sl] + chain(db, du, slope_s[:, sl], u, misc_s[0:1, sl])
        own_grad = own_grad - drel
        drels.append(drel)
    terms = [t.astype(f32) for t in split3(jnp.concatenate(drels, axis=1))]
    far = idx >= HALF
    terms = [jnp.where(far, 0.0, t) for t in terms] + [jnp.where(far, t, 0.0) for t in terms]
    spots = dot(jnp.concatenate(terms, axis=0).astype(bf16), oht[...], NT)
    spots = [spots[:8] + spots[8:16] + spots[16:24], spots[24:32] + spots[32:40] + spots[40:48]]
    for s in range(9):
        f_send[s] = spots[s // 5][:, (s % 5) * AT : (s % 5 + 1) * AT]
    copies = halo(3, lambda here: f_send.at[here], f_recv)
    pending += copies
    total = own_grad + f_send[4]
    for c in copies:
        c.wait_recv()
    for s in range(9):
        if s != 4:
            total = total + f_recv[s]
    force_ref[0, 0] = -(total[:3] + (2.0 * scale) * long_range[cq : cq + 3])

    for c in pending:
        c.wait_send()
    for k in range(KZ):
        pl.when(my != owners[k])(to_owner[k].wait_send)

    @pl.when(owning)
    def _():
        for c in spread:
            c.wait_send()

    for d in range(1, gx_n):
        back(d).wait_send()


def per_device(
    positions,
    species,
    neighbours,
    counts,
    species_embed,
    radial,
    mixing,
    read_hidden,
    read_out,
    charge_map,
    wavevectors,
):
    gx_n, gy_n = lax.axis_size("gx"), lax.axis_size("gy")
    rows = 2 * (charge_map.shape[1] // gx_n)
    vmem = pltpu.VMEM
    sem = pltpu.SemaphoreType.DMA
    scratch = [
        vmem((9, 8, AT), f32),
        vmem((gx_n, 8, AT), f32),
        vmem((9, C, AT), bf16),
        vmem((HALF, E), bf16),
        vmem((2 * C, HALF), bf16),
        vmem((NB, C, AT), bf16),
        vmem((NB, 2 * C, AT), f32),
        vmem((2 * C, E), bf16),
        vmem((8, E), f32),
        vmem((8, E), f32),
        vmem((8, E), f32),
        vmem((8, E), f32),
        vmem((8, E), f32),
        vmem((4, C, AT), f32),
        vmem((gx_n, LANES, AT), bf16),
        vmem((gx_n, LANES, AT), bf16),
        vmem((gx_n, KZ * rows, AT), f32),
        vmem((KZ * rows, LANES), f32),
        vmem((gx_n, rows, AT), f32),
        vmem((gx_n, rows, AT), f32),
        vmem((KZ, rows, LANES), f32),
        vmem((gy_n, rows, LANES), f32),
        vmem((rows, LANES), f32),
        vmem((KZ, rows, LANES), f32),
        vmem((gx_n, 8, AT), f32),
        vmem((gx_n, 8, AT), f32),
        vmem((9, C, AT), bf16),
        vmem((9, C, AT), bf16),
        vmem((9, 8, AT), f32),
        vmem((9, 8, AT), f32),
        sem((4, 9)),
        sem((4, 9)),
        sem((3, gx_n)),
        sem((3, gx_n)),
        sem((KZ,)),
        sem((gy_n,)),
        sem((gy_n,)),
        sem((KZ,)),
    ]
    return pl.pallas_call(
        functools.partial(kernel, gx_n, gy_n),
        out_shape=(
            jax.ShapeDtypeStruct((1, 1, 3, AT), f32),
            jax.ShapeDtypeStruct((1, 1, AT), f32),
        ),
        in_specs=[pl.BlockSpec(memory_space=pltpu.VMEM)] * 11,
        out_specs=(pl.BlockSpec(memory_space=pltpu.VMEM),) * 2,
        scratch_shapes=scratch,
        compiler_params=pltpu.CompilerParams(
            collective_id=0, has_side_effects=True, vmem_limit_bytes=60 * 1024 * 1024
        ),
    )(
        positions,
        species,
        neighbours[0, 0].T,
        counts,
        species_embed,
        radial,
        mixing,
        read_hidden,
        read_out[None],
        charge_map,
        wavevectors,
    )


def solution(mesh):
    in_specs = (
        P("gx", "gy", None, None),
        P("gx", "gy", None),
        P("gx", "gy", None, None),
        P("gx", "gy", None),
        P(),
        P(),
        P(),
        P(),
        P(),
        P(),
        P(),
    )
    out_specs = (P("gx", "gy", None, None), P("gx", "gy", None))
    return jax.shard_map(
        per_device, mesh=mesh, in_specs=in_specs, out_specs=out_specs, check_vma=False
    )
```

```python
import functools
import math

import jax
import jax.numpy as jnp
from jax import lax
from jax.experimental import pallas as pl
from jax.experimental.pallas import tpu as pltpu
from jax.sharding import PartitionSpec as P

MESH = pl.DeviceIdType.MESH
f32, bf16 = jnp.float32, jnp.bfloat16
NN, NT, TN = ((1,), (0,)), ((1,), (1,)), ((0,), (0,))
CELL, HEIGHT, CUT = 10.0, 30.0, 50.0
AT, NB, C, NR, NS = 256, 12, 128, 8, 6
E = AT * NB
HALF = 1280
KZ = 9
LANES = 384
DEPTH = 896
UNROLL = 4
NORM = 1.0 / math.sqrt(NB)


def dot(a, b, dims):
    return lax.dot_general(a, b, (dims, ((), ())), preferred_element_type=f32)


def split2(x):
    hi = x.astype(bf16)
    return hi, (x - hi.astype(f32)).astype(bf16)


def split3(x):
    hi = x.astype(bf16)
    rest = x - hi.astype(f32)
    mid = rest.astype(bf16)
    return hi, mid, (rest - mid.astype(f32)).astype(bf16)


def dot3(a, b, dims):
    ah, al = split2(a)
    bh, bl = split2(b)
    return dot(ah, bh, dims) + dot(ah, bl, dims) + dot(al, bh, dims)


def rowid(shape):
    return lax.broadcasted_iota(jnp.int32, shape, 0)


def laneid(shape):
    return lax.broadcasted_iota(jnp.int32, shape, 1)


def sigmoid(x):
    return 1.0 / (1.0 + jnp.exp(-x))


def silu_pair(x):
    s = sigmoid(x)
    return x * s, s * (1.0 + x * (1.0 - s))


def swap_rows(x):
    h = x.shape[0] // 2
    return jnp.concatenate([x[h:], x[:h]], axis=0)


def shift_lanes(x, by):
    by = by % x.shape[1]
    return jnp.concatenate([x[:, -by:], x[:, :-by]], axis=1)


def swap_sixteens(x):
    return jnp.where(laneid(x.shape) < 16, shift_lanes(x, -16), shift_lanes(x, 16))


def colsum(x):
    return jnp.sum(x, axis=0, keepdims=True)


def one_hot(idx_row):
    f = jnp.where(idx_row >= HALF, idx_row - HALF, idx_row)
    return jnp.where(rowid((HALF, AT)) == f, 1.0, 0.0).astype(bf16)


def pos_table(frame):
    cells = []
    for s in range(9):
        a, b = divmod(s, 3)
        r = rowid((8, AT))
        shift = jnp.where(r == 0, CELL * (a - 1), 0.0) + jnp.where(r == 1, CELL * (b - 1), 0.0)
        cells.append(frame[s] + shift)
    cells.append(jnp.zeros((8, AT), f32))
    parts = []
    for half in (cells[:5], cells[5:]):
        parts += [t.astype(f32) for t in split3(jnp.concatenate(half, axis=1))]
    return jnp.concatenate(parts, axis=0).astype(bf16)


def geometry(gathered, idx, own, cnt):
    low = gathered[0:8] + gathered[8:16] + gathered[16:24]
    high = gathered[24:32] + gathered[32:40] + gathered[40:48]
    pos = jnp.where(idx >= HALF, high, low)
    rel = jnp.where(rowid((8, E)) < 3, pos - jnp.concatenate([own] * NB, axis=1), 0.0)
    kind = pos[3:4]
    dist = jnp.sqrt(colsum(rel * rel) + 0.25)
    inv = 1.0 / dist
    unit = rel * inv
    freq = (rowid((8, 1)) + 1).astype(f32) * (math.pi / CUT)
    arg = dist * freq
    live = jnp.concatenate([jnp.where(n < cnt, 1.0, 0.0) for n in range(NB)], axis=1)
    basis = jnp.sin(arg) / arg
    slope = (jnp.cos(arg) - basis) * (inv * live)
    return basis * live, slope, unit, inv, kind


def chain(db, du, slope, unit, inv):
    return du * inv + unit * (colsum(db * slope) - inv * colsum(du * unit))


def kind_rows(kind):
    return jnp.where(rowid((8, AT)).astype(f32) == kind, 1.0, 0.0).astype(bf16)


def embed_cols(embed8, kind):
    oh = kind_rows(kind)
    hi, mid, lo = split3(embed8)
    return dot(hi, oh, TN) + dot(mid, oh, TN) + dot(lo, oh, TN)


def first_sums(basis, unit, kind):
    sums = [jnp.zeros((32, AT), f32) for _ in range(NS)]
    for n in range(NB):
        sl = slice(n * AT, (n + 1) * AT)
        b, u, k = basis[:, sl], unit[:, sl], kind[:, sl]
        z = jnp.concatenate([b, b * u[0:1], b * u[1:2], b * u[2:3]], axis=0)
        for s in range(NS):
            sums[s] = sums[s] + jnp.where(k == float(s), z, 0.0)
    return [jnp.concatenate([t[8 * p : 8 * p + 8] for t in sums], axis=0) for p in range(4)]


def pair_rows(radial, embed8):
    return jnp.concatenate([radial * embed8[s : s + 1] for s in range(NS)], axis=0)


def layer_one(sums, own_kind, radial0, radial1, mix0, mix1, embed8):
    re0, re1 = pair_rows(radial0, embed8), pair_rows(radial1, embed8)
    m0 = dot3(re0, sums[0], TN) * NORM
    m1 = dot3(re1, jnp.concatenate(sums[1:], axis=1), TN) * NORM
    mx = [m1[:, p * AT : (p + 1) * AT] for p in range(3)]
    sq = mx[0] * mx[0] + mx[1] * mx[1] + mx[2] * mx[2]
    act, slope = silu_pair(dot3(mix0, m0, TN) + dot3(mix1, sq, TN))
    return embed_cols(embed8, own_kind) + act, slope, m1


def layer_one_back(grad, slope, m1, radial0, radial1, mix0, mix1, embed8):
    re0, re1 = pair_rows(radial0, embed8), pair_rows(radial1, embed8)
    dpre = grad * slope
    d0 = dot3(mix0, dpre, NN) * NORM
    dsq = dot3(mix1, dpre, NN) * (2.0 * NORM)
    d1 = m1 * jnp.concatenate([dsq] * 3, axis=1)
    a0 = dot3(re0, d0, NN)
    a1 = dot3(re1, d1, NN)
    return [a0] + [a1[:, p * AT : (p + 1) * AT] for p in range(3)]


def first_sums_back(n, sums, basis, unit, kind):
    z = []
    for t in sums:
        got = jnp.zeros((8, AT), f32)
        for s in range(NS):
            got = jnp.where(kind == float(s), t[8 * s : 8 * s + 8], got)
        z.append(got)
    db = z[0] + z[1] * unit[0:1] + z[2] * unit[1:2] + z[3] * unit[2:3]
    du = [colsum(basis * t) for t in z[1:]]
    return db, jnp.concatenate(du + [jnp.zeros((5, AT), f32)], axis=0)


def radial_left(radial0, radial1):
    r = jnp.concatenate([radial0, radial1], axis=1)
    hi, lo = split2(r)
    hi, lo = hi.astype(f32), lo.astype(f32)
    return jnp.concatenate([hi, hi, lo, jnp.zeros_like(hi)], axis=0).T.astype(bf16)


def basis_right(b):
    hi, lo = split2(b)
    hi, lo = hi.astype(f32), lo.astype(f32)
    return jnp.concatenate([hi, lo, hi, jnp.zeros_like(hi)], axis=0).astype(bf16)


def second_slot(folded, oh, idx_row, left, b):
    both = dot(folded, oh, NN)
    g = jnp.where(idx_row >= HALF, both[C:], both[:C])
    return g, dot(left, basis_right(b), NN)


def second_slot_back(g, w, idx_row, unit, d0, d1, rhi, rstack):
    w0, w1 = w[:C], w[C:]
    ux, uy, uz = unit[0:1], unit[1:2], unit[2:3]
    p = d1[0] * ux + d1[1] * uy + d1[2] * uz
    dg = w0 * d0 + w1 * p
    xh, xl = split2(jnp.concatenate([g * d0, g * p], axis=0))
    both = dot(rstack, xh, NN)
    db = both[:8] + both[8:] + dot(rhi, xl, NN)
    t = w1 * g
    du = [colsum(t * d) for d in d1]
    du = jnp.concatenate(du + [jnp.zeros((5, AT), f32)], axis=0)
    far = idx_row >= HALF
    dgm = jnp.concatenate([jnp.where(far, 0.0, dg), jnp.where(far, dg, 0.0)], axis=0)
    return dgm, db, du


def trig8(pos_row, origin, length):
    theta = (pos_row + origin) * (2.0 * math.pi / length)
    arg = theta * (rowid((8, 1)) + 1).astype(f32)
    return jnp.cos(arg), jnp.sin(arg)


def phases(pos, ox, oy, lx, ly, cq):
    c1, s1 = trig8(pos[0:1], ox, lx)
    c2, s2 = trig8(pos[1:2], oy, ly)
    c3, s3 = trig8(pos[2:3], 0.0, HEIGHT)
    cos, sin = [], []
    for m in range(8):
        a, b = c1[m : m + 1], s1[m : m + 1]
        cc, ss, sc, cs = a * c2, b * s2, b * c2, a * s2
        cos += [cc - ss, cc + ss]
        sin += [sc + cs, sc - cs]
    main = jnp.concatenate(cos + sin, axis=0)
    rest = jnp.concatenate([c1, c2, s1, s2], axis=0)
    third = [jnp.where(rowid((2 * cq, AT)) < cq, 1.0, 0.0)]
    for m in range(8):
        third.append(jnp.where(rowid((2 * cq, AT)) < cq, c3[m : m + 1], s3[m : m + 1]))
    return main, rest, jnp.concatenate(third, axis=0)


def phase_rows(main, rest):
    mh, ml = split2(main)
    rh, rl = (t.astype(f32) for t in split2(rest))
    tail = jnp.concatenate([rh, rh, rl, jnp.zeros_like(rh)], axis=0).astype(bf16)
    return mh, ml, tail


def structure_cell(third, q2, mh, ml, tail):
    n = third.shape[0]
    qh, ql = split2(third * jnp.concatenate([q2] * KZ, axis=0))
    qq = jnp.concatenate([qh, ql], axis=0)
    both = dot(qq, mh, NT)
    return both[:n] + both[n:] + dot(qh, ml, NT), dot(qq, tail, NT)


def join_rest(both):
    n = both.shape[0] // 2
    return both[:n] + both[n:] + shift_lanes(both[:n], -64)


def fold_depth(left):
    hi, lo = split2(left)
    rh, rl = hi[:, 256:].astype(f32), lo[:, 256:].astype(f32)
    tail = (rh + shift_lanes(rl, 32) + shift_lanes(rh, 64)).astype(bf16)
    return jnp.concatenate([hi[:, :256], lo[:, :256], hi[:, :256], tail], axis=1)


def wave_cols(waves):
    k1, k2, k3 = waves[0:1], waves[1:2], waves[2:3]
    flip = (k1 < 0) | ((k1 == 0) & (k2 < 0))
    k1, k2, k3 = (jnp.where(flip, -k, k) for k in (k1, k2, k3))
    main = (k1 - 1) * 16 + jnp.where(k2 > 0, k2 - 1, 7 - k2)
    col = jnp.where(k1 == 0, 135 + k2, jnp.where(k2 == 0, 127 + k1, main))
    return col, k3


def count_part(col, k3, kappa):
    oh = jnp.where(rowid((256, AT)) == col, 1.0, 0.0).astype(bf16)
    r = rowid((8, AT))
    want = jnp.where(r == 0, kappa, jnp.where(r == 1, -kappa, 99))
    return dot(jnp.where(k3 == want, 1.0, 0.0).astype(bf16), oh, NT)


def col_numbers():
    lane = laneid((1, 256))
    low = (lane & 7) + 1
    k1 = jnp.where(lane < 128, (lane >> 4) + 1, jnp.where(lane < 136, low, 0))
    k2 = jnp.where(lane < 128, jnp.where((lane & 15) < 8, low, -low), jnp.where(lane < 136, 0, low))
    k1, k2 = jnp.where(lane < 144, k1, 0), jnp.where(lane < 144, k2, 0)
    return k1.astype(f32), k2.astype(f32)


def widen(x):
    main, rest = x[:, :128], x[:, 128:]
    rest = rest + shift_lanes(rest, 16)
    return jnp.concatenate([main, main, rest], axis=1)


def weights(count, kappa, lx, ly):
    k1, k2 = col_numbers()
    kz = kappa.astype(f32)
    wx, wy, wz = 2.0 * math.pi * k1 / lx, 2.0 * math.pi * k2 / ly, 2.0 * math.pi * kz / HEIGHT
    sq = wx * wx + wy * wy + wz * wz
    green = jnp.exp(-0.5 * sq) / (sq + 0.25)
    plus = count[0:1] * green
    minus = jnp.where(kappa == 0, 0.0, count[1:2] * green)
    return widen(plus + minus), widen(plus - minus)


def turn(t, sign):
    rest = t[:, 256:]
    swapped = swap_sixteens(rest)
    rest = jnp.where(laneid(rest.shape) < 16, sign * swapped, -sign * swapped)
    return jnp.concatenate([sign * t[:, 128:256], -sign * t[:, :128], rest], axis=1)


def weigh(t, sigma, delta):
    cq = t.shape[0] // 2
    sign = jnp.where(rowid((2 * cq, 1)) < cq, -1.0, 1.0)
    return sigma * t + delta * turn(swap_rows(t), sign)


def fold_left(v, lx, ly):
    k1, k2 = col_numbers()
    kx, ky = widen(k1) * (2.0 * math.pi / lx), widen(k2) * (2.0 * math.pi / ly)
    t = turn(v, 1.0)
    return jnp.concatenate([v, kx * t, ky * t], axis=0)


def fold_cell(u, third, q):
    cq = q.shape[0]
    rows = KZ * 2 * cq
    zero = jnp.zeros((2 * cq, AT), f32)
    pot, gx, gy, gz = zero, zero, zero, zero
    for k in range(KZ):
        at = slice(k * 2 * cq, (k + 1) * 2 * cq)
        t, part = third[at], u[at]
        pot = pot + t * part
        gx = gx + t * u[rows:][at]
        gy = gy + t * u[2 * rows :][at]
        if k:
            gz = gz + swap_rows(t) * (part * (2.0 * math.pi * k / HEIGHT))
    qq = jnp.concatenate([q, q], axis=0)
    sign = jnp.where(rowid((2 * cq, 1)) < cq, -1.0, 1.0)
    rows = [pot[:cq] + pot[cq:], colsum(qq * gx), colsum(qq * gy), colsum(qq * gz * sign)]
    return jnp.concatenate(rows + [jnp.zeros((1, AT), f32)], axis=0)


def kernel(
    gx_n,
    gy_n,
    pos_ref,
    kind_ref,
    nbr_ref,
    cnt_ref,
    emb_ref,
    rad_ref,
    mix_ref,
    rh_ref,
    ro_ref,
    cm_ref,
    wave_ref,
    force_ref,
    site_ref,
    pfr,
    prow,
    hfr,
    oht,
    gfold,
    g_s,
    w_s,
    dgm_s,
    drel_s,
    basis_s,
    slope_s,
    unit_s,
    misc_s,
    m_s,
    ph,
    tr,
    t_s,
    u_s,
    lk,
    q_send,
    q_recv,
    t_send,
    t_recv,
    v_send,
    v_all,
    b_send,
    b_recv,
    g_send,
    g_recv,
    f_send,
    f_recv,
    halo_s,
    halo_r,
    row_s,
    row_r,
    red_s,
    red_r,
    bc_s,
    bc_r,
):
    mx, my = lax.axis_index("gx"), lax.axis_index("gy")
    cq = cm_ref.shape[0] // gx_n
    lx, ly = CELL * gx_n, CELL * gy_n
    atoms_all = AT * gx_n * gy_n
    scale = 1.0 / math.sqrt(wave_ref.shape[1] * cm_ref.shape[0] * atoms_all)

    def cell(da, db):
        return lax.rem(mx + da + gx_n, gx_n), lax.rem(my + db + gy_n, gy_n)

    around = [(da, db) for da in (-1, 0, 1) for db in (-1, 0, 1) if (da, db) != (0, 0)]
    around.sort(key=lambda t: -abs(t[0]) - abs(t[1]))
    far_col = sorted(range(1, gy_n), key=lambda d: -min(d % 4, 4 - d % 4) - min(d // 4, 4 - d // 4))
    far_row = sorted(range(1, gx_n), key=lambda d: -min(d, gx_n - d))

    def remote(src, dst, ssem, rsem, dev):
        return pltpu.make_async_remote_copy(
            src_ref=src,
            dst_ref=dst,
            send_sem=ssem,
            recv_sem=rsem,
            device_id=dev,
            device_id_type=MESH,
        )

    def halo(stage, src_of, dst_of, pick=None):
        copies = []
        for da, db in around if pick is None else pick:
            here, there = 3 * (da + 1) + db + 1, 3 * (1 - da) + 1 - db
            copies.append(
                remote(
                    src_of(here),
                    dst_of(there),
                    halo_s.at[stage, here],
                    halo_r.at[stage, there],
                    cell(da, db),
                )
            )
            copies[-1].start()
        return copies

    pending = []
    pfr[...] = jnp.zeros_like(pfr)

    barrier = pltpu.get_barrier_semaphore()
    mates = [cell(d, 0) for d in range(1, gx_n)] + [cell(0, d) for d in range(1, gy_n)]
    mates += [cell(da, db) for da, db in around if da and db]
    for dev in mates:
        pl.semaphore_signal(barrier, inc=1, device_id=dev, device_id_type=MESH)

    row = rowid((8, AT))
    own = jnp.where(row == 3, kind_ref[0].astype(f32), 0.0)
    for p in range(3):
        own = jnp.where(row == p, pos_ref[p], own)
    pfr[4] = own
    prow[0] = own
    pl.semaphore_wait(barrier, len(mates))

    copies = halo(0, lambda here: pfr.at[4, :4], lambda there: pfr.at[there, :4])
    row_pos = [
        remote(prow.at[0, :3], prow.at[d, :3], row_s.at[0, d], row_r.at[0, d], cell(d, 0))
        for d in far_row
    ]
    for c in row_pos:
        c.start()
    pending += copies + row_pos

    def slot(n):
        return pl.ds(pl.multiple_of(n * AT, AT), AT)

    def hot(n, _):
        oht[:, slot(n)] = one_hot(nbr_ref[n])
        return 0

    lax.fori_loop(0, NB, hot, 0)
    embed8 = jnp.zeros((8, C), f32)
    for s in range(NS):
        embed8 = jnp.where(rowid((8, C)) == s, emb_ref[s : s + 1, :], embed8)
    idx = jnp.concatenate([nbr_ref[n] for n in range(NB)], axis=1)
    for c in copies:
        c.wait_recv()

    gathered = dot(pos_table([pfr[s] for s in range(9)]), oht[...], NN)
    basis, slope, unit, inv, kind = geometry(gathered, idx, own, cnt_ref[0])
    basis_s[...] = basis
    slope_s[...] = slope
    unit_s[...] = unit
    misc_s[0:1] = inv
    misc_s[1:2] = kind
    layer = (rad_ref[0, 0], rad_ref[0, 1], mix_ref[0, 0], mix_ref[0, 1], embed8)
    hidden, slope1, m1_first = layer_one(first_sums(basis, unit, kind), own[3:4], *layer)
    hfr[4] = hidden.astype(bf16)
    copies = halo(1, lambda here: hfr.at[4], lambda there: hfr.at[there])
    pending += copies

    for c in row_pos:
        c.wait_recv()

    def phase(d, _):
        source = lax.rem(mx - d + gx_n, gx_n)
        main, rest, third = phases(
            prow[d], source.astype(f32) * CELL, my.astype(f32) * CELL, lx, ly, cq
        )
        mh, ml, tail = phase_rows(main, rest)
        ph[d, 0:256] = mh
        ph[d, 256:512] = mh
        ph[d, 512:768] = ml
        ph[d, 768:] = tail
        tr[d] = third
        return 0

    lax.fori_loop(0, gx_n, phase, 0, unroll=UNROLL)
    owners = [k * gy_n // KZ for k in range(KZ)]

    def owned(j):
        k = (j * KZ + gy_n - 1) // gy_n
        takes = (k < KZ) & ((k * gy_n) // KZ == j)
        return jnp.minimum(k, KZ - 1), takes

    kappa, owning = owned(my)

    def count(s, total):
        col, k3 = wave_cols(wave_ref[:, slot(s)])
        return total + count_part(col, k3, kappa)

    counted = jnp.zeros((8, AT), f32)
    counted = lax.fori_loop(0, wave_ref.shape[1] // AT, count, counted, unroll=UNROLL)
    sigma, delta = weights(counted, kappa, lx, ly)
    left = radial_left(rad_ref[1, 0], rad_ref[1, 1])
    for c in copies:
        c.wait_recv()

    for s in range(9):
        part = slice(0, C) if s < 5 else slice(C, 2 * C)
        gfold[part, (s % 5) * AT : (s % 5 + 1) * AT] = hfr[s]
    gfold[C:, 4 * AT :] = jnp.zeros((C, AT), bf16)
    m_s[...] = jnp.zeros_like(m_s)

    def forward(n, _):
        g, w = second_slot(
            gfold[...], oht[:, slot(n)], nbr_ref[n], left, basis_s[:, slot(n)]
        )
        g_s[n] = g.astype(bf16)
        w_s[n] = w
        u = unit_s[:, slot(n)]
        m_s[0] += w[:C] * g
        t = w[C:] * g
        for p in range(3):
            m_s[1 + p] += t * u[p : p + 1]
        return 0

    lax.fori_loop(0, NB, forward, 0, unroll=UNROLL)
    m1 = [m_s[1 + p] * NORM for p in range(3)]
    sq = m1[0] * m1[0] + m1[1] * m1[1] + m1[2] * m1[2]
    act, slope2 = silu_pair(
        dot3(mix_ref[1, 0], m_s[0] * NORM, TN) + dot3(mix_ref[1, 1], sq, TN)
    )
    h2 = hfr[4].astype(f32) + act
    q = dot3(cm_ref[...], h2, NN)
    for p in range(gx_n):
        q_send[p] = jnp.concatenate([q[cq * p : cq * p + cq]] * 2, axis=0)
    q_recv[0] = q_send[mx]
    q_copies = {}
    for d in far_row:
        dev = cell(d, 0)
        q_copies[d] = remote(
            q_send.at[dev[0], :cq], q_recv.at[d, :cq], row_s.at[1, d], row_r.at[1, d], dev
        )
        q_copies[d].start()
    pending += q_copies.values()
    r, rs = silu_pair(dot3(rh_ref[...], h2, TN))
    ro8 = jnp.broadcast_to(ro_ref[...], (8, C))
    energy = dot3(ro8, r, NN)[0:1]
    dread = dot3(rh_ref[...] * ro_ref[...], rs, NN)

    t_s[...] = jnp.zeros_like(t_s)
    u_s[...] = jnp.zeros_like(u_s)
    near = [0] + far_row[::-1]
    for at in range(0, gx_n, UNROLL):
        for d in near[at : at + UNROLL]:
            if d:
                q_copies[d].wait_recv()
        for d in near[at : at + UNROLL]:
            q2 = jnp.concatenate([q_recv[d, :cq]] * 2, axis=0)
            main, rest = structure_cell(tr[d], q2, ph[d, 0:256], ph[d, 512:768], ph[d, 768:])
            t_s[...] += main
            u_s[...] += rest
    rows = 2 * cq
    rest = join_rest(u_s[...])
    for k in range(KZ):
        t_send[k, :, :256] = t_s[k * rows : (k + 1) * rows, :]
        t_send[k, :, 256:] = rest[k * rows : (k + 1) * rows]
    to_owner = []
    for d in far_col:
        dev = cell(0, d)
        k, takes = owned(dev[1])
        copy = remote(t_send.at[k], t_recv.at[my], red_s.at[d], red_r.at[my], dev)
        to_owner.append((takes, copy))
        pl.when(takes)(copy.start)

    spread = [
        remote(v_send, v_all.at[kappa], bc_s.at[d], bc_r.at[kappa], cell(0, d)) for d in far_col
    ]

    @pl.when(owning)
    def _():
        t_recv[my] = t_send[kappa]
        for d in range(1, gy_n):
            src = lax.rem(my + d, gy_n)
            remote(
                t_send.at[0], t_recv.at[src], red_s.at[1], red_r.at[src], (mx, src)
            ).wait_recv()
        total = t_recv[0]
        for j in range(1, gy_n):
            total = total + t_recv[j]
        v = weigh(total, sigma, delta)
        v_send[...] = v
        v_all[kappa] = v
        for c in spread:
            c.start()

    for k in range(KZ):
        arrive = remote(v_send, v_all.at[k], bc_s.at[0], bc_r.at[k], (mx, owners[k]))
        pl.when(my != owners[k])(arrive.wait_recv)

    v = jnp.concatenate([v_all[k] for k in range(KZ)], axis=0)
    lk[...] = fold_depth(fold_left(v, lx, ly))

    def back(d):
        dev = cell(-d, 0)
        return remote(
            b_send.at[d, : cq + 3], b_recv.at[mx, : cq + 3], row_s.at[2, d], row_r.at[2, d], dev
        )

    order = far_row + [0]
    for at in range(0, gx_n, UNROLL):
        for d in order[at : at + UNROLL]:
            b_send[d] = fold_cell(dot(lk[...], ph[d], NN), tr[d], q_recv[d, :cq])
        for d in order[at : at + UNROLL]:
            if d:
                back(d).start()
    b_recv[mx] = b_send[0]
    for d in range(1, gx_n):
        src = lax.rem(mx + d, gx_n)
        remote(
            b_send.at[d, : cq + 3],
            b_recv.at[src, : cq + 3],
            row_s.at[2, d],
            row_r.at[2, d],
            (src, my),
        ).wait_recv()
    pot = jnp.concatenate([b_recv[p, :cq] for p in range(gx_n)], axis=0)
    long_range = b_recv[0, cq : cq + 3]
    for p in range(1, gx_n):
        long_range = long_range + b_recv[p, cq : cq + 3]
    site_ref[0] = energy + scale * colsum(q * pot)

    dh = dread + dot3(cm_ref[...], pot * (2.0 * scale), TN)
    dpre = dh * slope2
    d0 = dot3(mix_ref[1, 0], dpre, NN) * NORM
    dsq = dot3(mix_ref[1, 1], dpre, NN) * (2.0 * NORM)
    m_s[0] = d0
    for p in range(3):
        m_s[1 + p] = m1[p] * dsq
    rhi, rlo = split2(jnp.concatenate([rad_ref[1, 0], rad_ref[1, 1]], axis=1))
    rstack = jnp.concatenate([rhi.astype(f32), rlo.astype(f32)], axis=0).astype(bf16)

    def backward(n, _):
        u = unit_s[:, slot(n)]
        dgm, db, du = second_slot_back(
            g_s[n].astype(f32),
            w_s[n],
            nbr_ref[n],
            u,
            m_s[0],
            [m_s[1], m_s[2], m_s[3]],
            rhi,
            rstack,
        )
        dgm_s[:, slot(n)] = dgm.astype(bf16)
        drel_s[:, slot(n)] = chain(db, du, slope_s[:, slot(n)], u, misc_s[0:1, slot(n)])
        return 0

    lax.fori_loop(0, NB, backward, 0, unroll=UNROLL)
    copies = []
    for t in range(5):
        part = dot(dgm_s[...], oht[t * AT : (t + 1) * AT, :], NT)
        if t == 4:
            grad = dh + part[:C]
            break
        for s, value in ((t, part[:C]), (t + 5, part[C:])):
            g_send[s] = value.astype(bf16)
            copies += halo(
                2, lambda h: g_send.at[h], lambda h: g_recv.at[h], [(s // 3 - 1, s % 3 - 1)]
            )
    pending += copies
    for c in copies:
        c.wait_recv()
    for s in range(9):
        if s != 4:
            grad = grad + g_recv[s].astype(f32)

    sums = layer_one_back(grad, slope1, m1_first, *layer)
    own_grad = jnp.zeros((8, AT), f32)
    drels = []
    for n in range(NB):
        sl = slice(n * AT, (n + 1) * AT)
        b, u = basis_s[:, sl], unit_s[:, sl]
        db, du = first_sums_back(n, sums, b, u, misc_s[1:2, sl])
        drel = drel_s[:, sl] + chain(db, du, slope_s[:, sl], u, misc_s[0:1, sl])
        own_grad = own_grad - drel
        drels.append(drel)
    terms = [t.astype(f32) for t in split3(jnp.concatenate(drels, axis=1))]
    far = idx >= HALF
    terms = [jnp.where(far, 0.0, t) for t in terms] + [jnp.where(far, t, 0.0) for t in terms]
    terms = jnp.concatenate(terms, axis=0).astype(bf16)
    copies = []
    for t in range(5):
        part = dot(terms, oht[t * AT : (t + 1) * AT, :], NT)
        low = part[:8] + part[8:16] + part[16:24]
        if t == 4:
            total = own_grad + low
            break
        for s, value in ((t, low), (t + 5, part[24:32] + part[32:40] + part[40:48])):
            f_send[s] = value
            copies += halo(
                3,
                lambda h: f_send.at[h, :3],
                lambda h: f_recv.at[h, :3],
                [(s // 3 - 1, s % 3 - 1)],
            )
    pending += copies
    total = total[:3]
    for c in copies:
        c.wait_recv()
    for s in range(9):
        if s != 4:
            total = total + f_recv[s, :3]
    total = -(total + (2.0 * scale) * long_range)
    for p in range(3):
        force_ref[p] = total[p : p + 1]

    for c in pending:
        c.wait_send()
    for takes, copy in to_owner:
        pl.when(takes)(copy.wait_send)

    @pl.when(owning)
    def _():
        for c in spread:
            c.wait_send()

    for d in range(1, gx_n):
        back(d).wait_send()


def per_device(
    positions,
    species,
    neighbours,
    counts,
    species_embed,
    radial,
    mixing,
    read_hidden,
    read_out,
    charge_map,
    wavevectors,
):
    gx_n, gy_n = lax.axis_size("gx"), lax.axis_size("gy")
    rows = 2 * (charge_map.shape[1] // gx_n)
    vmem = pltpu.VMEM
    sem = pltpu.SemaphoreType.DMA
    scratch = [
        vmem((9, 8, AT), f32),
        vmem((gx_n, 8, AT), f32),
        vmem((9, C, AT), bf16),
        vmem((HALF, E), bf16),
        vmem((2 * C, HALF), bf16),
        vmem((NB, C, AT), bf16),
        vmem((NB, 2 * C, AT), f32),
        vmem((2 * C, E), bf16),
        vmem((8, E), f32),
        vmem((8, E), f32),
        vmem((8, E), f32),
        vmem((8, E), f32),
        vmem((8, E), f32),
        vmem((4, C, AT), f32),
        vmem((gx_n, DEPTH, AT), bf16),
        vmem((gx_n, KZ * rows, AT), f32),
        vmem((KZ * rows, 256), f32),
        vmem((2 * KZ * rows, 128), f32),
        vmem((3 * KZ * rows, DEPTH), bf16),
        vmem((gx_n, rows, AT), f32),
        vmem((gx_n, rows, AT), f32),
        vmem((KZ, rows, LANES), f32),
        vmem((gy_n, rows, LANES), f32),
        vmem((rows, LANES), f32),
        vmem((KZ, rows, LANES), f32),
        vmem((gx_n, 8, AT), f32),
        vmem((gx_n, 8, AT), f32),
        vmem((9, C, AT), bf16),
        vmem((9, C, AT), bf16),
        vmem((9, 8, AT), f32),
        vmem((9, 8, AT), f32),
        sem((4, 9)),
        sem((4, 9)),
        sem((3, gx_n)),
        sem((3, gx_n)),
        sem((gy_n,)),
        sem((gy_n,)),
        sem((gy_n,)),
        sem((KZ,)),
    ]
    forces, site_energy = pl.pallas_call(
        functools.partial(kernel, gx_n, gy_n),
        out_shape=(
            jax.ShapeDtypeStruct((3, 1, AT), f32),
            jax.ShapeDtypeStruct((1, 1, AT), f32),
        ),
        in_specs=[pl.BlockSpec(memory_space=pltpu.VMEM)] * 11,
        out_specs=(pl.BlockSpec(memory_space=pltpu.VMEM),) * 2,
        scratch_shapes=scratch,
        compiler_params=pltpu.CompilerParams(
            collective_id=0, has_side_effects=True, vmem_limit_bytes=60 * 1024 * 1024
        ),
    )(
        jnp.transpose(positions[0], (1, 0, 2)),
        species,
        jnp.transpose(neighbours[0], (2, 0, 1)),
        counts,
        species_embed,
        radial,
        mixing,
        read_hidden,
        read_out[None],
        charge_map.T,
        wavevectors,
    )
    return jnp.transpose(forces, (1, 0, 2))[None], site_energy


def solution(mesh):
    in_specs = (
        P("gx", "gy", None, None),
        P("gx", "gy", None),
        P("gx", "gy", None, None),
        P("gx", "gy", None),
        P(),
        P(),
        P(),
        P(),
        P(),
        P(),
        P(),
    )
    out_specs = (P("gx", "gy", None, None), P("gx", "gy", None))
    return jax.shard_map(
        per_device, mesh=mesh, in_specs=in_specs, out_specs=out_specs, check_vma=False
    )
```

```python
import functools
import math

import jax
import jax.numpy as jnp
from jax import lax
from jax.experimental import pallas as pl
from jax.experimental.pallas import tpu as pltpu
from jax.sharding import PartitionSpec as P

MESH = pl.DeviceIdType.MESH
f32, bf16 = jnp.float32, jnp.bfloat16
NN, NT, TN = ((1,), (0,)), ((1,), (1,)), ((0,), (0,))
CELL, HEIGHT, CUT = 10.0, 30.0, 50.0
AT, NB, C, NR, NS = 256, 12, 128, 8, 6
E = AT * NB
HALF = 1280
KZ = 9
LANES = 384
DEPTH = 896
UNROLL = 4
NORM = 1.0 / math.sqrt(NB)
TILES = ((4, None), (1, 7), (3, 5), (0, 2), (6, 8))
NEAR = 3 * AT


def dot(a, b, dims):
    return lax.dot_general(a, b, (dims, ((), ())), preferred_element_type=f32)


def split2(x):
    hi = x.astype(bf16)
    return hi, (x - hi.astype(f32)).astype(bf16)


def split3(x):
    hi = x.astype(bf16)
    rest = x - hi.astype(f32)
    mid = rest.astype(bf16)
    return hi, mid, (rest - mid.astype(f32)).astype(bf16)


def dot3(a, b, dims):
    ah, al = split2(a)
    bh, bl = split2(b)
    return dot(ah, bh, dims) + dot(ah, bl, dims) + dot(al, bh, dims)


def dot3s(a, b):
    bh, bl = split2(b)
    return dot(a[0], bh, NN) + dot(a[0], bl, NN) + dot(a[1], bh, NN)


def rowid(shape):
    return lax.broadcasted_iota(jnp.int32, shape, 0)


def laneid(shape):
    return lax.broadcasted_iota(jnp.int32, shape, 1)


def sigmoid(x):
    return 1.0 / (1.0 + jnp.exp(-x))


def silu_pair(x):
    s = sigmoid(x)
    return x * s, s * (1.0 + x * (1.0 - s))


def swap_rows(x):
    h = x.shape[0] // 2
    return jnp.concatenate([x[h:], x[:h]], axis=0)


def shift_lanes(x, by):
    by = by % x.shape[1]
    return jnp.concatenate([x[:, -by:], x[:, :-by]], axis=1)


def swap_sixteens(x):
    return jnp.where(laneid(x.shape) < 16, shift_lanes(x, -16), shift_lanes(x, 16))


def colsum(x):
    return jnp.sum(x, axis=0, keepdims=True)


def folded(idx_row):
    which = idx_row >> 8
    tile, far = jnp.zeros_like(idx_row), jnp.zeros_like(idx_row)
    for t, pair in enumerate(TILES[1:], 1):
        tile = jnp.where((which == pair[0]) | (which == pair[1]), t, tile)
        far = jnp.where(which == pair[1], 1, far)
    return tile * AT + (idx_row & (AT - 1)), far


def one_hot(f):
    return jnp.where(rowid((HALF, AT)) == f, 1.0, 0.0).astype(bf16)


def pos_table(frame, tiles):
    parts = []
    for side in range(2):
        cells = []
        for pair in tiles:
            s = pair[side]
            if s is None:
                cells.append(jnp.zeros((8, AT), f32))
                continue
            a, b = divmod(s, 3)
            r = rowid((8, AT))
            shift = jnp.where(r == 0, CELL * (a - 1), 0.0) + jnp.where(r == 1, CELL * (b - 1), 0.0)
            cells.append(frame[s] + shift)
        parts += [t.astype(f32) for t in split3(jnp.concatenate(cells, axis=1))]
    return jnp.concatenate(parts, axis=0).astype(bf16)


def geometry(gathered, far, own, cnt):
    low = gathered[0:8] + gathered[8:16] + gathered[16:24]
    high = gathered[24:32] + gathered[32:40] + gathered[40:48]
    pos = jnp.where(far > 0, high, low)
    rel = jnp.where(rowid((8, E)) < 3, pos - jnp.concatenate([own] * NB, axis=1), 0.0)
    kind = pos[3:4]
    dist = jnp.sqrt(colsum(rel * rel) + 0.25)
    inv = 1.0 / dist
    unit = rel * inv
    freq = (rowid((8, 1)) + 1).astype(f32) * (math.pi / CUT)
    arg = dist * freq
    live = jnp.concatenate([jnp.where(n < cnt, 1.0, 0.0) for n in range(NB)], axis=1)
    basis = jnp.sin(arg) / arg
    slope = (jnp.cos(arg) - basis) * (inv * live)
    return basis * live, slope, unit, inv, kind


def chain(db, du, slope, unit, inv):
    return du * inv + unit * (colsum(db * slope) - inv * colsum(du * unit))


def kind_rows(kind):
    return jnp.where(rowid((8, AT)).astype(f32) == kind, 1.0, 0.0).astype(bf16)


def embed_cols(embed8, kind):
    oh = kind_rows(kind)
    hi, mid, lo = split3(embed8)
    return dot(hi, oh, TN) + dot(mid, oh, TN) + dot(lo, oh, TN)


def first_sums(basis, unit, kind):
    sums = [jnp.zeros((32, AT), f32) for _ in range(NS)]
    for n in range(NB):
        sl = slice(n * AT, (n + 1) * AT)
        b, u, k = basis[:, sl], unit[:, sl], kind[:, sl]
        z = jnp.concatenate([b, b * u[0:1], b * u[1:2], b * u[2:3]], axis=0)
        for s in range(NS):
            sums[s] = sums[s] + jnp.where(k == float(s), z, 0.0)
    return [jnp.concatenate([t[8 * p : 8 * p + 8] for t in sums], axis=0) for p in range(4)]


def pair_rows(radial, embed8):
    return jnp.concatenate([radial * embed8[s : s + 1] for s in range(NS)], axis=0)


def layer_one(sums, initial, re0, re1, mix0, mix1):
    m0 = dot3s(re0, sums[0]) * NORM
    m1 = dot3s(re1, jnp.concatenate(sums[1:], axis=1)) * NORM
    mx = [m1[:, p * AT : (p + 1) * AT] for p in range(3)]
    sq = mx[0] * mx[0] + mx[1] * mx[1] + mx[2] * mx[2]
    act, slope = silu_pair(dot3s(mix0, m0) + dot3s(mix1, sq))
    return initial + act, slope, m1


def layer_one_back(grad, slope, m1, re0, re1, mix0, mix1):
    dpre = grad * slope
    d0 = dot3s(mix0, dpre) * NORM
    dsq = dot3s(mix1, dpre) * (2.0 * NORM)
    d1 = m1 * jnp.concatenate([dsq] * 3, axis=1)
    a0 = dot3s(re0, d0)
    a1 = dot3s(re1, d1)
    return [a0] + [a1[:, p * AT : (p + 1) * AT] for p in range(3)]


def first_sums_back(n, sums, basis, unit, kind):
    z = []
    for t in sums:
        got = jnp.zeros((8, AT), f32)
        for s in range(NS):
            got = jnp.where(kind == float(s), t[8 * s : 8 * s + 8], got)
        z.append(got)
    db = z[0] + z[1] * unit[0:1] + z[2] * unit[1:2] + z[3] * unit[2:3]
    du = [colsum(basis * t) for t in z[1:]]
    return db, jnp.concatenate(du + [jnp.zeros((5, AT), f32)], axis=0)


def radial_left(radial0, radial1):
    r = jnp.concatenate([radial0, radial1], axis=1)
    hi, lo = split2(r)
    hi, lo = hi.astype(f32), lo.astype(f32)
    return jnp.concatenate([hi, hi, lo, jnp.zeros_like(hi)], axis=0).T.astype(bf16)


def basis_right(b):
    hi, lo = split2(b)
    hi, lo = hi.astype(f32), lo.astype(f32)
    return jnp.concatenate([hi, lo, hi, jnp.zeros_like(hi)], axis=0).astype(bf16)


def second_slot_back(g, w, far, unit, d0, d1, rhi, rstack):
    w0, w1 = w[:C], w[C:]
    ux, uy, uz = unit[0:1], unit[1:2], unit[2:3]
    p = d1[0] * ux + d1[1] * uy + d1[2] * uz
    dg = w0 * d0 + w1 * p
    xh, xl = split2(jnp.concatenate([g * d0, g * p], axis=0))
    both = dot(rstack, xh, NN)
    db = both[:8] + both[8:] + dot(rhi, xl, NN)
    t = w1 * g
    du = [colsum(t * d) for d in d1]
    du = jnp.concatenate(du + [jnp.zeros((5, AT), f32)], axis=0)
    far = far > 0
    dgm = jnp.concatenate([jnp.where(far, 0.0, dg), jnp.where(far, dg, 0.0)], axis=0)
    return dgm, db, du


def trig8(pos_row, origin, length):
    theta = (pos_row + origin) * (2.0 * math.pi / length)
    arg = theta * (rowid((8, 1)) + 1).astype(f32)
    return jnp.cos(arg), jnp.sin(arg)


def phases(pos, ox, oy, lx, ly, cq):
    c1, s1 = trig8(pos[0:1], ox, lx)
    c2, s2 = trig8(pos[1:2], oy, ly)
    c3, s3 = trig8(pos[2:3], 0.0, HEIGHT)
    cos, sin = [], []
    for m in range(8):
        a, b = c1[m : m + 1], s1[m : m + 1]
        cc, ss, sc, cs = a * c2, b * s2, b * c2, a * s2
        cos += [cc - ss, cc + ss]
        sin += [sc + cs, sc - cs]
    main = jnp.concatenate(cos + sin, axis=0)
    rest = jnp.concatenate([c1, c2, s1, s2], axis=0)
    third = [jnp.where(rowid((2 * cq, AT)) < cq, 1.0, 0.0)]
    for m in range(8):
        third.append(jnp.where(rowid((2 * cq, AT)) < cq, c3[m : m + 1], s3[m : m + 1]))
    return main, rest, jnp.concatenate(third, axis=0)


def phase_rows(main, rest):
    mh, ml = split2(main)
    rh, rl = (t.astype(f32) for t in split2(rest))
    tail = jnp.concatenate([rh, rh, rl, jnp.zeros_like(rh)], axis=0).astype(bf16)
    return mh, ml, tail


def structure_cell(third, q2, mh, ml, tail):
    n = third.shape[0]
    qh, ql = split2(third * jnp.concatenate([q2] * KZ, axis=0))
    qq = jnp.concatenate([qh, ql], axis=0)
    both = dot(qq, mh, NT)
    return both[:n] + both[n:] + dot(qh, ml, NT), dot(qq, tail, NT)


def join_rest(both):
    n = both.shape[0] // 2
    return both[:n] + both[n:] + shift_lanes(both[:n], -64)


def fold_depth(left):
    hi, lo = split2(left)
    rh, rl = hi[:, 256:].astype(f32), lo[:, 256:].astype(f32)
    tail = (rh + shift_lanes(rl, 32) + shift_lanes(rh, 64)).astype(bf16)
    return jnp.concatenate([hi[:, :256], lo[:, :256], hi[:, :256], tail], axis=1)


def wave_cols(waves):
    k1, k2, k3 = waves[0:1], waves[1:2], waves[2:3]
    flip = (k1 < 0) | ((k1 == 0) & (k2 < 0))
    k1, k2, k3 = (jnp.where(flip, -k, k) for k in (k1, k2, k3))
    main = (k1 - 1) * 16 + jnp.where(k2 > 0, k2 - 1, 7 - k2)
    col = jnp.where(k1 == 0, 135 + k2, jnp.where(k2 == 0, 127 + k1, main))
    return col, k3


def count_part(col, k3, kappa):
    oh = jnp.where(rowid((256, AT)) == col, 1.0, 0.0).astype(bf16)
    r = rowid((8, AT))
    want = jnp.where(r == 0, kappa, jnp.where(r == 1, -kappa, 99))
    return dot(jnp.where(k3 == want, 1.0, 0.0).astype(bf16), oh, NT)


def col_numbers():
    lane = laneid((1, 256))
    low = (lane & 7) + 1
    k1 = jnp.where(lane < 128, (lane >> 4) + 1, jnp.where(lane < 136, low, 0))
    k2 = jnp.where(lane < 128, jnp.where((lane & 15) < 8, low, -low), jnp.where(lane < 136, 0, low))
    k1, k2 = jnp.where(lane < 144, k1, 0), jnp.where(lane < 144, k2, 0)
    return k1.astype(f32), k2.astype(f32)


def widen(x):
    main, rest = x[:, :128], x[:, 128:]
    rest = rest + shift_lanes(rest, 16)
    return jnp.concatenate([main, main, rest], axis=1)


def weights(count, kappa, lx, ly):
    k1, k2 = col_numbers()
    kz = kappa.astype(f32)
    wx, wy, wz = 2.0 * math.pi * k1 / lx, 2.0 * math.pi * k2 / ly, 2.0 * math.pi * kz / HEIGHT
    sq = wx * wx + wy * wy + wz * wz
    green = jnp.exp(-0.5 * sq) / (sq + 0.25)
    plus = count[0:1] * green
    minus = jnp.where(kappa == 0, 0.0, count[1:2] * green)
    return widen(plus + minus), widen(plus - minus)


def turn(t, sign):
    rest = t[:, 256:]
    swapped = swap_sixteens(rest)
    rest = jnp.where(laneid(rest.shape) < 16, sign * swapped, -sign * swapped)
    return jnp.concatenate([sign * t[:, 128:256], -sign * t[:, :128], rest], axis=1)


def weigh(t, sigma, delta):
    cq = t.shape[0] // 2
    sign = jnp.where(rowid((2 * cq, 1)) < cq, -1.0, 1.0)
    return sigma * t + delta * turn(swap_rows(t), sign)


def fold_left(v, lx, ly):
    k1, k2 = col_numbers()
    kx, ky = widen(k1) * (2.0 * math.pi / lx), widen(k2) * (2.0 * math.pi / ly)
    t = turn(v, 1.0)
    return jnp.concatenate([v, kx * t, ky * t], axis=0)


def fold_cell(u, third, q):
    cq = q.shape[0]
    rows = KZ * 2 * cq
    zero = jnp.zeros((2 * cq, AT), f32)
    pot, gx, gy, gz = zero, zero, zero, zero
    for k in range(KZ):
        at = slice(k * 2 * cq, (k + 1) * 2 * cq)
        t, part = third[at], u[at]
        pot = pot + t * part
        gx = gx + t * u[rows:][at]
        gy = gy + t * u[2 * rows :][at]
        if k:
            gz = gz + swap_rows(t) * (part * (2.0 * math.pi * k / HEIGHT))
    qq = jnp.concatenate([q, q], axis=0)
    sign = jnp.where(rowid((2 * cq, 1)) < cq, -1.0, 1.0)
    rows = [pot[:cq] + pot[cq:], colsum(qq * gx), colsum(qq * gy), colsum(qq * gz * sign)]
    return jnp.concatenate(rows + [jnp.zeros((1, AT), f32)], axis=0)


def kernel(
    gx_n,
    gy_n,
    *refs,
):
    arrays, (force_ref, site_ref), rest = refs[:11], refs[11:13], refs[13:]
    kept, load_s, rest = rest[:11], rest[11], rest[12:]
    pos_ref, kind_ref, nbr_ref, cnt_ref, emb_ref, rad_ref, mix_ref, rh_ref = kept[:8]
    ro_ref, cm_ref, wave_ref = kept[8:]
    (
        pfr, prow, hfr, oht, half_s, fold_s, part_s, gp_s, gfold, g_s, w_s, dgm_s,
        drel_s, basis_s, slope_s, unit_s, misc_s, m_s, ph, tr, t_s, u_s, lk, q_send,
        q_recv, t_send, t_recv, v_send, v_all, b_send, b_recv, g_send, g_recv, f_send,
        f_recv, halo_s, halo_r, row_s, row_r, red_s, red_r, bc_s, bc_r,
    ) = rest
    mx, my = lax.axis_index("gx"), lax.axis_index("gy")
    cq = cm_ref.shape[0] // gx_n
    lx, ly = CELL * gx_n, CELL * gy_n
    atoms_all = AT * gx_n * gy_n
    scale = 1.0 / math.sqrt(wave_ref.shape[1] * cm_ref.shape[0] * atoms_all)

    def cell(da, db):
        return lax.rem(mx + da + gx_n, gx_n), lax.rem(my + db + gy_n, gy_n)

    around = [(da, db) for da in (-1, 0, 1) for db in (-1, 0, 1) if (da, db) != (0, 0)]
    around.sort(key=lambda t: -abs(t[0]) - abs(t[1]))
    far_col = sorted(range(1, gy_n), key=lambda d: -min(d % 4, 4 - d % 4) - min(d // 4, 4 - d // 4))
    far_row = sorted(range(1, gx_n), key=lambda d: -min(d, gx_n - d))

    def remote(src, dst, ssem, rsem, dev):
        return pltpu.make_async_remote_copy(
            src_ref=src,
            dst_ref=dst,
            send_sem=ssem,
            recv_sem=rsem,
            device_id=dev,
            device_id_type=MESH,
        )

    def halo(stage, src_of, dst_of, pick=None):
        copies = []
        for da, db in around if pick is None else pick:
            here, there = 3 * (da + 1) + db + 1, 3 * (1 - da) + 1 - db
            copies.append(
                remote(
                    src_of(here),
                    dst_of(there),
                    halo_s.at[stage, here],
                    halo_r.at[stage, there],
                    cell(da, db),
                )
            )
            copies[-1].start()
        return copies

    pending = []
    pfr[...] = jnp.zeros_like(pfr)
    loads = [
        pltpu.make_async_copy(a, k, load_s.at[i]) for i, (a, k) in enumerate(zip(arrays, kept))
    ]

    barrier = pltpu.get_barrier_semaphore()
    mates = [cell(d, 0) for d in range(1, gx_n)] + [cell(0, d) for d in range(1, gy_n)]
    mates += [cell(da, db) for da, db in around if da and db]
    for dev in mates:
        pl.semaphore_signal(barrier, inc=1, device_id=dev, device_id_type=MESH)

    for c in loads:
        c.start()
    for c in loads[:2]:
        c.wait()
    row = rowid((8, AT))
    own = jnp.where(row == 3, kind_ref[0].astype(f32), 0.0)
    for p in range(3):
        own = jnp.where(row == p, pos_ref[p], own)
    pfr[4] = own
    prow[0] = own
    pl.semaphore_wait(barrier, len(mates))

    copies = halo(0, lambda here: pfr.at[4, :4], lambda there: pfr.at[there, :4])
    row_pos = [
        remote(prow.at[0, :3], prow.at[d, :3], row_s.at[0, d], row_r.at[0, d], cell(d, 0))
        for d in far_row
    ]
    for c in row_pos:
        c.start()
    pending += copies + row_pos
    for c in loads[2:]:
        c.wait()

    def slot(n):
        return pl.ds(pl.multiple_of(n * AT, AT), AT)

    def hot(n, _):
        f, far = folded(nbr_ref[n])
        fold_s[n] = f
        half_s[n] = far
        oht[:, slot(n)] = one_hot(f)
        return 0

    lax.fori_loop(0, NB, hot, 0)
    embed8 = jnp.zeros((8, C), f32)
    for s in range(NS):
        embed8 = jnp.where(rowid((8, C)) == s, emb_ref[s : s + 1, :], embed8)
    far = jnp.concatenate([half_s[n] for n in range(NB)], axis=1)
    initial = embed_cols(embed8, own[3:4])
    pairs = [pair_rows(rad_ref[0, p], embed8) for p in range(2)]
    turned = [split2(m.T) for m in pairs + [mix_ref[0, 0], mix_ref[0, 1]]]
    for c in copies[4:]:
        c.wait_recv()
    gp_s[...] = dot(pos_table(pfr, TILES[:3]), oht[:NEAR, :], NN)
    for c in copies[:4]:
        c.wait_recv()

    gathered = gp_s[...] + dot(pos_table(pfr, TILES[3:]), oht[NEAR:, :], NN)
    basis, slope, unit, inv, kind = geometry(gathered, far, own, cnt_ref[0])
    basis_s[...] = basis
    slope_s[...] = slope
    unit_s[...] = unit
    misc_s[0:1] = inv
    misc_s[1:2] = kind
    hidden, slope1, m1_first = layer_one(first_sums(basis, unit, kind), initial, *turned)
    hfr[4] = hidden.astype(bf16)
    side = 1 - 2 * lax.rem(mx, 2)
    outer, inner = 3 * (1 - side), 3 * (1 + side)

    def feature(src, dst, sem_at, dev):
        return remote(hfr.at[src], hfr.at[dst], halo_s.at[1, sem_at], halo_r.at[1, dst], dev)

    along_y = [feature(4, 4 - e, 4 + e, cell(0, e)) for e in (-1, 1)]
    corners = [feature(4, inner + 1 - e, 1 + e, cell(-side, e)) for e in (-1, 1)]
    along_x = [feature(4, 4 - 3 * e, 4 + 3 * e, cell(e, 0)) for e in (-1, 1)]
    for c in along_y + corners + along_x:
        c.start()
    pending += along_y + corners + along_x

    for c in row_pos:
        c.wait_recv()

    def phase(d, _):
        source = lax.rem(mx - d + gx_n, gx_n)
        main, rest, third = phases(
            prow[d], source.astype(f32) * CELL, my.astype(f32) * CELL, lx, ly, cq
        )
        mh, ml, tail = phase_rows(main, rest)
        ph[d, 0:256] = mh
        ph[d, 256:512] = mh
        ph[d, 512:768] = ml
        ph[d, 768:] = tail
        tr[d] = third
        return 0

    lax.fori_loop(0, gx_n, phase, 0, unroll=UNROLL)
    owners = [k * gy_n // KZ for k in range(KZ)]

    def owned(j):
        k = (j * KZ + gy_n - 1) // gy_n
        takes = (k < KZ) & ((k * gy_n) // KZ == j)
        return jnp.minimum(k, KZ - 1), takes

    kappa, owning = owned(my)

    def count(s, total):
        col, k3 = wave_cols(wave_ref[:, slot(s)])
        return total + count_part(col, k3, kappa)

    counted = jnp.zeros((8, AT), f32)
    counted = lax.fori_loop(0, wave_ref.shape[1] // AT, count, counted, unroll=UNROLL)
    sigma, delta = weights(counted, kappa, lx, ly)
    left = radial_left(rad_ref[1, 0], rad_ref[1, 1])

    def frame_tile(t):
        for side, cell_at in enumerate(TILES[t]):
            if cell_at is not None:
                gfold[side * C : side * C + C, t * AT : (t + 1) * AT] = hfr[cell_at]

    mix_turned = [split2(mix_ref[1, p].T) for p in range(2)]
    cm_split, rh_turned = split2(cm_ref[...]), split2(rh_ref[...].T)
    gfold[C:, :AT] = jnp.zeros((C, AT), bf16)
    m_s[...] = jnp.zeros_like(m_s)
    passed = []
    for c, e in zip(along_y, (-1, 1)):
        c.wait_recv()
        passed.append(feature(4 - e, outer + 1 - e, 7 + e, cell(side, 0)))
        passed[-1].start()
    pending += passed
    for c in along_x:
        c.wait_recv()
    for t in range(3):
        frame_tile(t)

    def near_part(n, _):
        part_s[n] = dot(gfold[:, :NEAR], oht[:NEAR, slot(n)], NN)
        w_s[n] = dot(left, basis_right(basis_s[:, slot(n)]), NN)
        return 0

    lax.fori_loop(0, NB, near_part, 0, unroll=UNROLL)
    for e in (-1, 1):
        feature(4, outer + 1 + e, 1 + e, cell(0, e)).wait_recv()
        feature(4, inner + 1 + e, 1 + e, cell(0, e)).wait_recv()
    for t in range(3, 5):
        frame_tile(t)

    def forward(n, _):
        both = part_s[n] + dot(gfold[:, NEAR:], oht[NEAR:, slot(n)], NN)
        g = jnp.where(half_s[n] > 0, both[C:], both[:C])
        g_s[n] = g.astype(bf16)
        w = w_s[n]
        u = unit_s[:, slot(n)]
        m_s[0] += w[:C] * g
        t = w[C:] * g
        for p in range(3):
            m_s[1 + p] += t * u[p : p + 1]
        return 0

    lax.fori_loop(0, NB, forward, 0, unroll=UNROLL)
    m1 = [m_s[1 + p] * NORM for p in range(3)]
    sq = m1[0] * m1[0] + m1[1] * m1[1] + m1[2] * m1[2]
    act, slope2 = silu_pair(
        dot3s(mix_turned[0], m_s[0] * NORM) + dot3s(mix_turned[1], sq)
    )
    h2 = hfr[4].astype(f32) + act
    q = dot3s(cm_split, h2)
    for p in range(gx_n):
        q_send[p, :cq] = q[cq * p : cq * p + cq]
    q_recv[0, :cq] = q_send[mx, :cq]
    q_copies = {}
    for d in far_row:
        dev = cell(d, 0)
        q_copies[d] = remote(
            q_send.at[dev[0], :cq], q_recv.at[d, :cq], row_s.at[1, d], row_r.at[1, d], dev
        )
        q_copies[d].start()
    pending += q_copies.values()
    r, rs = silu_pair(dot3s(rh_turned, h2))
    ro8 = jnp.broadcast_to(ro_ref[...], (8, C))
    energy = dot3(ro8, r, NN)[0:1]
    dread = dot3(rh_ref[...] * ro_ref[...], rs, NN)

    t_s[...] = jnp.zeros_like(t_s)
    u_s[...] = jnp.zeros_like(u_s)
    near = [0] + far_row[::-1]
    for at in range(0, gx_n, UNROLL):
        for d in near[at : at + UNROLL]:
            if d:
                q_copies[d].wait_recv()
        for d in near[at : at + UNROLL]:
            q2 = jnp.concatenate([q_recv[d, :cq]] * 2, axis=0)
            main, rest = structure_cell(tr[d], q2, ph[d, 0:256], ph[d, 512:768], ph[d, 768:])
            t_s[...] += main
            u_s[...] += rest
    rows = 2 * cq
    rest = join_rest(u_s[...])
    for k in range(KZ):
        t_send[k, :, :256] = t_s[k * rows : (k + 1) * rows, :]
        t_send[k, :, 256:] = rest[k * rows : (k + 1) * rows]
    to_owner = []
    for d in far_col:
        dev = cell(0, d)
        k, takes = owned(dev[1])
        copy = remote(t_send.at[k], t_recv.at[my], red_s.at[d], red_r.at[my], dev)
        to_owner.append((takes, copy))
        pl.when(takes)(copy.start)

    spread = [
        remote(v_send, v_all.at[kappa], bc_s.at[d], bc_r.at[kappa], cell(0, d)) for d in far_col
    ]

    @pl.when(owning)
    def _():
        t_recv[my] = t_send[kappa]
        for d in range(1, gy_n):
            src = lax.rem(my + d, gy_n)
            remote(
                t_send.at[0], t_recv.at[src], red_s.at[1], red_r.at[src], (mx, src)
            ).wait_recv()
        total = t_recv[0]
        for j in range(1, gy_n):
            total = total + t_recv[j]
        v = weigh(total, sigma, delta)
        v_send[...] = v
        v_all[kappa] = v
        for c in spread:
            c.start()

    for k in range(KZ):
        arrive = remote(v_send, v_all.at[k], bc_s.at[0], bc_r.at[k], (mx, owners[k]))
        pl.when(my != owners[k])(arrive.wait_recv)

    v = jnp.concatenate([v_all[k] for k in range(KZ)], axis=0)
    lk[...] = fold_depth(fold_left(v, lx, ly))

    def back(d):
        dev = cell(-d, 0)
        return remote(
            b_send.at[d, : cq + 3], b_recv.at[mx, : cq + 3], row_s.at[2, d], row_r.at[2, d], dev
        )

    order = far_row + [0]
    for at in range(0, gx_n, UNROLL):
        for d in order[at : at + UNROLL]:
            b_send[d] = fold_cell(dot(lk[...], ph[d], NN), tr[d], q_recv[d, :cq])
        for d in order[at : at + UNROLL]:
            if d:
                back(d).start()
    b_recv[mx] = b_send[0]
    cm_turned = split2(cm_ref[...].T)
    mix_split = [split2(mix_ref[1, p]) for p in range(2)]
    rhi, rlo = split2(jnp.concatenate([rad_ref[1, 0], rad_ref[1, 1]], axis=1))
    rstack = jnp.concatenate([rhi.astype(f32), rlo.astype(f32)], axis=0).astype(bf16)
    for d in range(1, gx_n):
        src = lax.rem(mx + d, gx_n)
        remote(
            b_send.at[d, : cq + 3],
            b_recv.at[src, : cq + 3],
            row_s.at[2, d],
            row_r.at[2, d],
            (src, my),
        ).wait_recv()
    pot = jnp.concatenate([b_recv[p, :cq] for p in range(gx_n)], axis=0)
    long_range = b_recv[0, cq : cq + 3]
    for p in range(1, gx_n):
        long_range = long_range + b_recv[p, cq : cq + 3]
    site_ref[0] = energy + scale * colsum(q * pot)

    dh = dread + dot3s(cm_turned, pot * (2.0 * scale))
    dpre = dh * slope2
    d0 = dot3s(mix_split[0], dpre) * NORM
    dsq = dot3s(mix_split[1], dpre) * (2.0 * NORM)
    m_s[0] = d0
    for p in range(3):
        m_s[1 + p] = m1[p] * dsq

    def backward(n, _):
        u = unit_s[:, slot(n)]
        dgm, db, du = second_slot_back(
            g_s[n].astype(f32),
            w_s[n],
            half_s[n],
            u,
            m_s[0],
            [m_s[1], m_s[2], m_s[3]],
            rhi,
            rstack,
        )
        dgm_s[:, slot(n)] = dgm.astype(bf16)
        drel_s[:, slot(n)] = chain(db, du, slope_s[:, slot(n)], u, misc_s[0:1, slot(n)])
        return 0

    lax.fori_loop(0, NB, backward, 0, unroll=UNROLL)

    def derivative(src, dst, sem_at, dev):
        return remote(g_send.at[src], g_recv.at[dst], halo_s.at[2, sem_at], halo_r.at[2, dst], dev)

    def spread_tile(t):
        return dot(dgm_s[...], oht[t * AT : (t + 1) * AT, :], NT)

    for t in (3, 4):
        part = spread_tile(t)
        g_send[TILES[t][0]] = part[:C].astype(bf16)
        g_send[TILES[t][1]] = part[C:].astype(bf16)
    shared = [derivative(inner + 1 + e, outer + 1 + e, 7 + e, cell(side, 0)) for e in (-1, 1)]
    corners = [derivative(outer + 1 + e, inner + 1 - e, 1 + e, cell(-side, e)) for e in (-1, 1)]
    for c in shared + corners:
        c.start()
    part = spread_tile(1)
    along_x = []
    for e, value in zip((-1, 1), (part[:C], part[C:])):
        g_send[4 + 3 * e] = value.astype(bf16)
        along_x.append(derivative(4 + 3 * e, 4 - 3 * e, 4 + 3 * e, cell(e, 0)))
        along_x[-1].start()
    part = spread_tile(2)
    along_y = []
    for e, value in zip((-1, 1), (part[:C], part[C:])):
        there = inner + 1 + e
        derivative(4, there, 7 + e, cell(side, 0)).wait_recv()
        g_send[4 + e] = (value + g_recv[there].astype(f32)).astype(bf16)
        along_y.append(derivative(4 + e, 4 - e, 4 + e, cell(0, e)))
        along_y[-1].start()
    pending += shared + corners + along_x + along_y
    grad = dh + spread_tile(0)[:C]
    pairs = [pair_rows(rad_ref[0, p], embed8) for p in range(2)]
    straight = [split2(m) for m in pairs + [mix_ref[0, 0], mix_ref[0, 1]]]
    for c in along_x + along_y:
        c.wait_recv()
    for e in (-1, 1):
        derivative(4, outer + 1 + e, 1 + e, cell(0, e)).wait_recv()
        grad = grad + g_recv[outer + 1 + e].astype(f32)
        grad = grad + g_recv[4 + e].astype(f32) + g_recv[4 + 3 * e].astype(f32)

    sums = layer_one_back(grad, slope1, m1_first, *straight)
    own_grad = jnp.zeros((8, AT), f32)
    drels = []
    for n in range(NB):
        sl = slice(n * AT, (n + 1) * AT)
        b, u = basis_s[:, sl], unit_s[:, sl]
        db, du = first_sums_back(n, sums, b, u, misc_s[1:2, sl])
        drel = drel_s[:, sl] + chain(db, du, slope_s[:, sl], u, misc_s[0:1, sl])
        own_grad = own_grad - drel
        drels.append(drel)
    terms = [t.astype(f32) for t in split3(jnp.concatenate(drels, axis=1))]
    second = far > 0
    terms = [jnp.where(second, 0.0, t) for t in terms] + [
        jnp.where(second, t, 0.0) for t in terms
    ]
    terms = jnp.concatenate(terms, axis=0).astype(bf16)
    copies = []
    for t in (3, 4, 2, 1, 0):
        part = dot(terms, oht[t * AT : (t + 1) * AT, :], NT)
        low = part[:8] + part[8:16] + part[16:24]
        if t == 0:
            total = own_grad + low
            break
        for s, value in zip(TILES[t], (low, part[24:32] + part[32:40] + part[40:48])):
            f_send[s] = value
            copies += halo(
                3,
                lambda h: f_send.at[h, :3],
                lambda h: f_recv.at[h, :3],
                [(s // 3 - 1, s % 3 - 1)],
            )
    pending += copies
    total = total[:3]
    for c in copies:
        c.wait_recv()
    for s in range(9):
        if s != 4:
            total = total + f_recv[s, :3]
    total = total + (2.0 * scale) * long_range
    for p in range(3):
        force_ref[p] = -total[p : p + 1]

    for c in pending:
        c.wait_send()
    for takes, copy in to_owner:
        pl.when(takes)(copy.wait_send)

    @pl.when(owning)
    def _():
        for c in spread:
            c.wait_send()

    for d in range(1, gx_n):
        back(d).wait_send()


def per_device(
    positions,
    species,
    neighbours,
    counts,
    species_embed,
    radial,
    mixing,
    read_hidden,
    read_out,
    charge_map,
    wavevectors,
):
    gx_n, gy_n = lax.axis_size("gx"), lax.axis_size("gy")
    rows = 2 * (charge_map.shape[1] // gx_n)
    vmem = pltpu.VMEM
    sem = pltpu.SemaphoreType.DMA
    scratch = [
        vmem((9, 8, AT), f32),
        vmem((gx_n, 8, AT), f32),
        vmem((9, C, AT), bf16),
        vmem((HALF, E), bf16),
        vmem((NB, 1, AT), jnp.int32),
        vmem((NB, 1, AT), jnp.int32),
        vmem((NB, 2 * C, AT), f32),
        vmem((48, E), f32),
        vmem((2 * C, HALF), bf16),
        vmem((NB, C, AT), bf16),
        vmem((NB, 2 * C, AT), f32),
        vmem((2 * C, E), bf16),
        vmem((8, E), f32),
        vmem((8, E), f32),
        vmem((8, E), f32),
        vmem((8, E), f32),
        vmem((8, E), f32),
        vmem((4, C, AT), f32),
        vmem((gx_n, DEPTH, AT), bf16),
        vmem((gx_n, KZ * rows, AT), f32),
        vmem((KZ * rows, 256), f32),
        vmem((2 * KZ * rows, 128), f32),
        vmem((3 * KZ * rows, DEPTH), bf16),
        vmem((gx_n, rows, AT), f32),
        vmem((gx_n, rows, AT), f32),
        vmem((KZ, rows, LANES), f32),
        vmem((gy_n, rows, LANES), f32),
        vmem((rows, LANES), f32),
        vmem((KZ, rows, LANES), f32),
        vmem((gx_n, 8, AT), f32),
        vmem((gx_n, 8, AT), f32),
        vmem((9, C, AT), bf16),
        vmem((9, C, AT), bf16),
        vmem((9, 8, AT), f32),
        vmem((9, 8, AT), f32),
        sem((4, 9)),
        sem((4, 9)),
        sem((3, gx_n)),
        sem((3, gx_n)),
        sem((gy_n,)),
        sem((gy_n,)),
        sem((gy_n,)),
        sem((KZ,)),
    ]
    arrays = (
        jnp.transpose(positions[0], (1, 0, 2)),
        species,
        jnp.transpose(neighbours[0], (2, 0, 1)),
        counts,
        species_embed,
        radial,
        mixing,
        read_hidden,
        read_out[None],
        charge_map.T,
        wavevectors,
    )
    forces, site_energy = pl.pallas_call(
        functools.partial(kernel, gx_n, gy_n),
        out_shape=(
            jax.ShapeDtypeStruct((3, 1, AT), f32),
            jax.ShapeDtypeStruct((1, 1, AT), f32),
        ),
        in_specs=[pl.BlockSpec(memory_space=pl.ANY)] * len(arrays),
        out_specs=(pl.BlockSpec(memory_space=pltpu.VMEM),) * 2,
        scratch_shapes=[vmem(a.shape, a.dtype) for a in arrays] + [sem((len(arrays),))] + scratch,
        compiler_params=pltpu.CompilerParams(
            collective_id=0, has_side_effects=True, vmem_limit_bytes=60 * 1024 * 1024
        ),
    )(*arrays)
    return jnp.transpose(forces, (1, 0, 2))[None], site_energy


def solution(mesh):
    in_specs = (
        P("gx", "gy", None, None),
        P("gx", "gy", None),
        P("gx", "gy", None, None),
        P("gx", "gy", None),
        P(),
        P(),
        P(),
        P(),
        P(),
        P(),
        P(),
    )
    out_specs = (P("gx", "gy", None, None), P("gx", "gy", None))
    return jax.shard_map(
        per_device, mesh=mesh, in_specs=in_specs, out_specs=out_specs, check_vma=False
    )
```

```python
import functools
import math

import jax
import jax.numpy as jnp
from jax import lax
from jax.experimental import pallas as pl
from jax.experimental.pallas import tpu as pltpu
from jax.sharding import PartitionSpec as P

MESH = pl.DeviceIdType.MESH
f32, bf16 = jnp.float32, jnp.bfloat16
NN, NT, TN = ((1,), (0,)), ((1,), (1,)), ((0,), (0,))
CELL, HEIGHT, CUT = 10.0, 30.0, 50.0
AT, NB, C, NR, NS = 256, 12, 128, 8, 6
E = AT * NB
HALF = 1280
KZ = 9
LANES = 384
DEPTH = 896
UNROLL = 4
NORM = 1.0 / math.sqrt(NB)
TILES = ((4, None), (1, 7), (3, 5), (0, 2), (6, 8))
NEAR = 3 * AT


def dot(a, b, dims):
    return lax.dot_general(a, b, (dims, ((), ())), preferred_element_type=f32)


def split2(x):
    hi = x.astype(bf16)
    return hi, (x - hi.astype(f32)).astype(bf16)


def split3(x):
    hi = x.astype(bf16)
    rest = x - hi.astype(f32)
    mid = rest.astype(bf16)
    return hi, mid, (rest - mid.astype(f32)).astype(bf16)


def dot3(a, b, dims):
    ah, al = split2(a)
    bh, bl = split2(b)
    return dot(ah, bh, dims) + dot(ah, bl, dims) + dot(al, bh, dims)


def dot3s(a, b):
    bh, bl = split2(b)
    return dot(a[0], bh, NN) + dot(a[0], bl, NN) + dot(a[1], bh, NN)


def rowid(shape):
    return lax.broadcasted_iota(jnp.int32, shape, 0)


def laneid(shape):
    return lax.broadcasted_iota(jnp.int32, shape, 1)


def sigmoid(x):
    return 1.0 / (1.0 + jnp.exp(-x))


def silu_pair(x):
    s = sigmoid(x)
    return x * s, s * (1.0 + x * (1.0 - s))


def swap_rows(x):
    h = x.shape[0] // 2
    return jnp.concatenate([x[h:], x[:h]], axis=0)


def shift_lanes(x, by):
    by = by % x.shape[1]
    return jnp.concatenate([x[:, -by:], x[:, :-by]], axis=1)


def swap_sixteens(x):
    return jnp.where(laneid(x.shape) < 16, shift_lanes(x, -16), shift_lanes(x, 16))


def colsum(x):
    return jnp.sum(x, axis=0, keepdims=True)


def folded(idx_row):
    which = idx_row >> 8
    tile, far = jnp.zeros_like(idx_row), jnp.zeros_like(idx_row)
    for t, pair in enumerate(TILES[1:], 1):
        tile = jnp.where((which == pair[0]) | (which == pair[1]), t, tile)
        far = jnp.where(which == pair[1], 1, far)
    return tile * AT + (idx_row & (AT - 1)), far


def one_hot(f):
    return jnp.where(rowid((HALF, AT)) == f, 1.0, 0.0).astype(bf16)


def pos_table(frame, tiles):
    parts = []
    for side in range(2):
        cells = []
        for pair in tiles:
            s = pair[side]
            if s is None:
                cells.append(jnp.zeros((8, AT), f32))
                continue
            a, b = divmod(s, 3)
            r = rowid((8, AT))
            shift = jnp.where(r == 0, CELL * (a - 1), 0.0) + jnp.where(r == 1, CELL * (b - 1), 0.0)
            cells.append(frame[s] + shift)
        parts += [t.astype(f32) for t in split3(jnp.concatenate(cells, axis=1))]
    return jnp.concatenate(parts, axis=0).astype(bf16)


def geometry(gathered, far, own, cnt):
    low = gathered[0:8] + gathered[8:16] + gathered[16:24]
    high = gathered[24:32] + gathered[32:40] + gathered[40:48]
    pos = jnp.where(far > 0, high, low)
    rel = jnp.where(rowid((8, E)) < 3, pos - jnp.concatenate([own] * NB, axis=1), 0.0)
    kind = pos[3:4]
    dist = jnp.sqrt(colsum(rel * rel) + 0.25)
    inv = 1.0 / dist
    unit = rel * inv
    freq = (rowid((8, 1)) + 1).astype(f32) * (math.pi / CUT)
    arg = dist * freq
    live = jnp.concatenate([jnp.where(n < cnt, 1.0, 0.0) for n in range(NB)], axis=1)
    basis = jnp.sin(arg) / arg
    slope = (jnp.cos(arg) - basis) * (inv * live)
    return basis * live, slope, unit, inv, kind


def chain(db, du, slope, unit, inv):
    return du * inv + unit * (colsum(db * slope) - inv * colsum(du * unit))


def kind_rows(kind):
    return jnp.where(rowid((8, AT)).astype(f32) == kind, 1.0, 0.0).astype(bf16)


def embed_cols(embed8, kind):
    oh = kind_rows(kind)
    hi, mid, lo = split3(embed8)
    return dot(hi, oh, TN) + dot(mid, oh, TN) + dot(lo, oh, TN)


def first_sums(basis, unit, kind):
    sums = [jnp.zeros((32, AT), f32) for _ in range(NS)]
    for n in range(NB):
        sl = slice(n * AT, (n + 1) * AT)
        b, u, k = basis[:, sl], unit[:, sl], kind[:, sl]
        z = jnp.concatenate([b, b * u[0:1], b * u[1:2], b * u[2:3]], axis=0)
        for s in range(NS):
            sums[s] = sums[s] + jnp.where(k == float(s), z, 0.0)
    return [jnp.concatenate([t[8 * p : 8 * p + 8] for t in sums], axis=0) for p in range(4)]


def pair_rows(radial, embed8):
    return jnp.concatenate([radial * embed8[s : s + 1] for s in range(NS)], axis=0)


def layer_one(sums, initial, re0, re1, mix0, mix1):
    m0 = dot3s(re0, sums[0]) * NORM
    m1 = dot3s(re1, jnp.concatenate(sums[1:], axis=1)) * NORM
    mx = [m1[:, p * AT : (p + 1) * AT] for p in range(3)]
    sq = mx[0] * mx[0] + mx[1] * mx[1] + mx[2] * mx[2]
    act, slope = silu_pair(dot3s(mix0, m0) + dot3s(mix1, sq))
    return initial + act, slope, m1


def layer_one_back(grad, slope, m1, re0, re1, mix0, mix1):
    dpre = grad * slope
    d0 = dot3s(mix0, dpre) * NORM
    dsq = dot3s(mix1, dpre) * (2.0 * NORM)
    d1 = m1 * jnp.concatenate([dsq] * 3, axis=1)
    a0 = dot3s(re0, d0)
    a1 = dot3s(re1, d1)
    return [a0] + [a1[:, p * AT : (p + 1) * AT] for p in range(3)]


def first_sums_back(n, sums, basis, unit, kind):
    z = []
    for t in sums:
        got = jnp.zeros((8, AT), f32)
        for s in range(NS):
            got = jnp.where(kind == float(s), t[8 * s : 8 * s + 8], got)
        z.append(got)
    db = z[0] + z[1] * unit[0:1] + z[2] * unit[1:2] + z[3] * unit[2:3]
    du = [colsum(basis * t) for t in z[1:]]
    return db, jnp.concatenate(du + [jnp.zeros((5, AT), f32)], axis=0)


def radial_left(radial0, radial1):
    r = jnp.concatenate([radial0, radial1], axis=1)
    hi, lo = split2(r)
    hi, lo = hi.astype(f32), lo.astype(f32)
    return jnp.concatenate([hi, hi, lo, jnp.zeros_like(hi)], axis=0).T.astype(bf16)


def basis_right(b):
    hi, lo = split2(b)
    hi, lo = hi.astype(f32), lo.astype(f32)
    return jnp.concatenate([hi, lo, hi, jnp.zeros_like(hi)], axis=0).astype(bf16)


def second_slot_source(w, far, unit, d0, d1):
    p = d1[0] * unit[0:1] + d1[1] * unit[1:2] + d1[2] * unit[2:3]
    dg = w[:C] * d0 + w[C:] * p
    far = far > 0
    return jnp.concatenate([jnp.where(far, 0.0, dg), jnp.where(far, dg, 0.0)], axis=0)


def second_slot_back(g, w1, unit, d0, d1, rhi, rstack):
    p = d1[0] * unit[0:1] + d1[1] * unit[1:2] + d1[2] * unit[2:3]
    xh, xl = split2(jnp.concatenate([g * d0, g * p], axis=0))
    both = dot(rstack, xh, NN)
    db = both[:8] + both[8:] + dot(rhi, xl, NN)
    t = w1 * g
    du = [colsum(t * d) for d in d1]
    return db, jnp.concatenate(du + [jnp.zeros((5, AT), f32)], axis=0)


def trig8(pos_row, origin, length):
    theta = (pos_row + origin) * (2.0 * math.pi / length)
    arg = theta * (rowid((8, 1)) + 1).astype(f32)
    return jnp.cos(arg), jnp.sin(arg)


def phases(pos, ox, oy, lx, ly, cq):
    c1, s1 = trig8(pos[0:1], ox, lx)
    c2, s2 = trig8(pos[1:2], oy, ly)
    c3, s3 = trig8(pos[2:3], 0.0, HEIGHT)
    cos, sin = [], []
    for m in range(8):
        a, b = c1[m : m + 1], s1[m : m + 1]
        cc, ss, sc, cs = a * c2, b * s2, b * c2, a * s2
        cos += [cc - ss, cc + ss]
        sin += [sc + cs, sc - cs]
    main = jnp.concatenate(cos + sin, axis=0)
    rest = jnp.concatenate([c1, c2, s1, s2], axis=0)
    third = [jnp.where(rowid((2 * cq, AT)) < cq, 1.0, 0.0)]
    for m in range(8):
        third.append(jnp.where(rowid((2 * cq, AT)) < cq, c3[m : m + 1], s3[m : m + 1]))
    return main, rest, jnp.concatenate(third, axis=0)


def phase_rows(main, rest):
    mh, ml = split2(main)
    rh, rl = (t.astype(f32) for t in split2(rest))
    tail = jnp.concatenate([rh, rh, rl, jnp.zeros_like(rh)], axis=0).astype(bf16)
    return mh, ml, tail


def structure_cell(third, q2, mh, ml, tail):
    n = third.shape[0]
    qh, ql = split2(third * jnp.concatenate([q2] * KZ, axis=0))
    qq = jnp.concatenate([qh, ql], axis=0)
    both = dot(qq, mh, NT)
    return both[:n] + both[n:] + dot(qh, ml, NT), dot(qq, tail, NT)


def join_rest(both):
    n = both.shape[0] // 2
    return both[:n] + both[n:] + shift_lanes(both[:n], -64)


def fold_depth(left):
    hi, lo = split2(left)
    rh, rl = hi[:, 256:].astype(f32), lo[:, 256:].astype(f32)
    tail = (rh + shift_lanes(rl, 32) + shift_lanes(rh, 64)).astype(bf16)
    return jnp.concatenate([hi[:, :256], lo[:, :256], hi[:, :256], tail], axis=1)


def wave_cols(waves):
    k1, k2, k3 = waves[0:1], waves[1:2], waves[2:3]
    flip = (k1 < 0) | ((k1 == 0) & (k2 < 0))
    k1, k2, k3 = (jnp.where(flip, -k, k) for k in (k1, k2, k3))
    main = (k1 - 1) * 16 + jnp.where(k2 > 0, k2 - 1, 7 - k2)
    col = jnp.where(k1 == 0, 135 + k2, jnp.where(k2 == 0, 127 + k1, main))
    return col, k3


def count_part(col, k3, kappa):
    oh = jnp.where(rowid((256, AT)) == col, 1.0, 0.0).astype(bf16)
    r = rowid((8, AT))
    want = jnp.where(r == 0, kappa, jnp.where(r == 1, -kappa, 99))
    return dot(jnp.where(k3 == want, 1.0, 0.0).astype(bf16), oh, NT)


def col_numbers():
    lane = laneid((1, 256))
    low = (lane & 7) + 1
    k1 = jnp.where(lane < 128, (lane >> 4) + 1, jnp.where(lane < 136, low, 0))
    k2 = jnp.where(lane < 128, jnp.where((lane & 15) < 8, low, -low), jnp.where(lane < 136, 0, low))
    k1, k2 = jnp.where(lane < 144, k1, 0), jnp.where(lane < 144, k2, 0)
    return k1.astype(f32), k2.astype(f32)


def widen(x):
    main, rest = x[:, :128], x[:, 128:]
    rest = rest + shift_lanes(rest, 16)
    return jnp.concatenate([main, main, rest], axis=1)


def weights(count, kappa, lx, ly):
    k1, k2 = col_numbers()
    kz = kappa.astype(f32)
    wx, wy, wz = 2.0 * math.pi * k1 / lx, 2.0 * math.pi * k2 / ly, 2.0 * math.pi * kz / HEIGHT
    sq = wx * wx + wy * wy + wz * wz
    green = jnp.exp(-0.5 * sq) / (sq + 0.25)
    plus = count[0:1] * green
    minus = jnp.where(kappa == 0, 0.0, count[1:2] * green)
    return widen(plus + minus), widen(plus - minus)


def turn(t, sign):
    rest = t[:, 256:]
    swapped = swap_sixteens(rest)
    rest = jnp.where(laneid(rest.shape) < 16, sign * swapped, -sign * swapped)
    return jnp.concatenate([sign * t[:, 128:256], -sign * t[:, :128], rest], axis=1)


def weigh(t, sigma, delta):
    cq = t.shape[0] // 2
    sign = jnp.where(rowid((2 * cq, 1)) < cq, -1.0, 1.0)
    return sigma * t + delta * turn(swap_rows(t), sign)


def fold_left(v, lx, ly):
    k1, k2 = col_numbers()
    kx, ky = widen(k1) * (2.0 * math.pi / lx), widen(k2) * (2.0 * math.pi / ly)
    t = turn(v, 1.0)
    return jnp.concatenate([v, kx * t, ky * t], axis=0)


def fold_cell(u, third, q):
    cq = q.shape[0]
    rows = KZ * 2 * cq
    zero = jnp.zeros((2 * cq, AT), f32)
    pot, gx, gy, gz = zero, zero, zero, zero
    for k in range(KZ):
        at = slice(k * 2 * cq, (k + 1) * 2 * cq)
        t, part = third[at], u[at]
        pot = pot + t * part
        gx = gx + t * u[rows:][at]
        gy = gy + t * u[2 * rows :][at]
        if k:
            gz = gz + swap_rows(t) * (part * (2.0 * math.pi * k / HEIGHT))
    qq = jnp.concatenate([q, q], axis=0)
    sign = jnp.where(rowid((2 * cq, 1)) < cq, -1.0, 1.0)
    rows = [pot[:cq] + pot[cq:], colsum(qq * gx), colsum(qq * gy), colsum(qq * gz * sign)]
    return jnp.concatenate(rows + [jnp.zeros((1, AT), f32)], axis=0)


def kernel(
    gx_n,
    gy_n,
    *refs,
):
    arrays, (force_ref, site_ref), rest = refs[:11], refs[11:13], refs[13:]
    kept, load_s, rest = rest[:11], rest[11], rest[12:]
    pos_ref, kind_ref, nbr_ref, cnt_ref, emb_ref, rad_ref, mix_ref, rh_ref = kept[:8]
    ro_ref, cm_ref, wave_ref = kept[8:]
    (
        pfr, prow, hfr, oht, half_s, fold_s, part_s, gp_s, gfold, g_s, w_s, dgm_s,
        drel_s, basis_s, slope_s, unit_s, misc_s, m_s, ph, tr, t_s, u_s, lk, q_send,
        q_recv, t_send, t_recv, v_send, v_all, b_send, b_recv, g_send, g_recv, f_send,
        f_recv, halo_s, halo_r, row_s, row_r, red_s, red_r, bc_s, bc_r,
    ) = rest
    mx, my = lax.axis_index("gx"), lax.axis_index("gy")
    cq = cm_ref.shape[0] // gx_n
    lx, ly = CELL * gx_n, CELL * gy_n
    atoms_all = AT * gx_n * gy_n
    scale = 1.0 / math.sqrt(wave_ref.shape[1] * cm_ref.shape[0] * atoms_all)

    def cell(da, db):
        return lax.rem(mx + da + gx_n, gx_n), lax.rem(my + db + gy_n, gy_n)

    around = [(da, db) for da in (-1, 0, 1) for db in (-1, 0, 1) if (da, db) != (0, 0)]
    around.sort(key=lambda t: -abs(t[0]) - abs(t[1]))
    far_col = sorted(range(1, gy_n), key=lambda d: -min(d % 4, 4 - d % 4) - min(d // 4, 4 - d // 4))
    far_row = sorted(range(1, gx_n), key=lambda d: -min(d, gx_n - d))

    def remote(src, dst, ssem, rsem, dev):
        return pltpu.make_async_remote_copy(
            src_ref=src,
            dst_ref=dst,
            send_sem=ssem,
            recv_sem=rsem,
            device_id=dev,
            device_id_type=MESH,
        )

    def halo(stage, src_of, dst_of, pick=None):
        copies = []
        for da, db in around if pick is None else pick:
            here, there = 3 * (da + 1) + db + 1, 3 * (1 - da) + 1 - db
            copies.append(
                remote(
                    src_of(here),
                    dst_of(there),
                    halo_s.at[stage, here],
                    halo_r.at[stage, there],
                    cell(da, db),
                )
            )
            copies[-1].start()
        return copies

    pending = []
    pfr[...] = jnp.zeros_like(pfr)
    loads = [
        pltpu.make_async_copy(a, k, load_s.at[i]) for i, (a, k) in enumerate(zip(arrays, kept))
    ]

    barrier = pltpu.get_barrier_semaphore()
    mates = [cell(d, 0) for d in range(1, gx_n)] + [cell(0, d) for d in range(1, gy_n)]
    mates += [cell(da, db) for da, db in around if da and db]
    for dev in mates:
        pl.semaphore_signal(barrier, inc=1, device_id=dev, device_id_type=MESH)

    for c in loads:
        c.start()
    for c in loads[:2]:
        c.wait()
    row = rowid((8, AT))
    own = jnp.where(row == 3, kind_ref[0].astype(f32), 0.0)
    for p in range(3):
        own = jnp.where(row == p, pos_ref[p], own)
    pfr[4] = own
    prow[0] = own
    pl.semaphore_wait(barrier, len(mates))

    copies = halo(0, lambda here: pfr.at[4, :4], lambda there: pfr.at[there, :4])
    row_pos = [
        remote(prow.at[0, :3], prow.at[d, :3], row_s.at[0, d], row_r.at[0, d], cell(d, 0))
        for d in far_row
    ]
    for c in row_pos:
        c.start()
    pending += copies + row_pos
    for c in loads[2:]:
        c.wait()

    def slot(n):
        return pl.ds(pl.multiple_of(n * AT, AT), AT)

    def hot(n, _):
        f, far = folded(nbr_ref[n])
        fold_s[n] = f
        half_s[n] = far
        oht[:, slot(n)] = one_hot(f)
        return 0

    lax.fori_loop(0, NB, hot, 0)
    embed8 = jnp.zeros((8, C), f32)
    for s in range(NS):
        embed8 = jnp.where(rowid((8, C)) == s, emb_ref[s : s + 1, :], embed8)
    far = jnp.concatenate([half_s[n] for n in range(NB)], axis=1)
    initial = embed_cols(embed8, own[3:4])
    pairs = [pair_rows(rad_ref[0, p], embed8) for p in range(2)]
    turned = [split2(m.T) for m in pairs + [mix_ref[0, 0], mix_ref[0, 1]]]
    for c in copies[4:]:
        c.wait_recv()
    gp_s[...] = dot(pos_table(pfr, TILES[:3]), oht[:NEAR, :], NN)
    for c in copies[:4]:
        c.wait_recv()

    gathered = gp_s[...] + dot(pos_table(pfr, TILES[3:]), oht[NEAR:, :], NN)
    basis, slope, unit, inv, kind = geometry(gathered, far, own, cnt_ref[0])
    basis_s[...] = basis
    slope_s[...] = slope
    unit_s[...] = unit
    misc_s[0:1] = inv
    misc_s[1:2] = kind
    hidden, slope1, m1_first = layer_one(first_sums(basis, unit, kind), initial, *turned)
    hfr[4] = hidden.astype(bf16)
    side = 1 - 2 * lax.rem(mx, 2)
    outer, inner = 3 * (1 - side), 3 * (1 + side)

    def feature(src, dst, sem_at, dev):
        return remote(hfr.at[src], hfr.at[dst], halo_s.at[1, sem_at], halo_r.at[1, dst], dev)

    along_y = [feature(4, 4 - e, 4 + e, cell(0, e)) for e in (-1, 1)]
    corners = [feature(4, inner + 1 - e, 1 + e, cell(-side, e)) for e in (-1, 1)]
    along_x = [feature(4, 4 - 3 * e, 4 + 3 * e, cell(e, 0)) for e in (-1, 1)]
    for c in along_y + corners + along_x:
        c.start()
    pending += along_y + corners + along_x

    for c in row_pos:
        c.wait_recv()

    def phase(d, _):
        source = lax.rem(mx - d + gx_n, gx_n)
        main, rest, third = phases(
            prow[d], source.astype(f32) * CELL, my.astype(f32) * CELL, lx, ly, cq
        )
        mh, ml, tail = phase_rows(main, rest)
        ph[d, 0:256] = mh
        ph[d, 256:512] = mh
        ph[d, 512:768] = ml
        ph[d, 768:] = tail
        tr[d] = third
        return 0

    lax.fori_loop(0, gx_n, phase, 0, unroll=UNROLL)
    owners = [k * gy_n // KZ for k in range(KZ)]

    def owned(j):
        k = (j * KZ + gy_n - 1) // gy_n
        takes = (k < KZ) & ((k * gy_n) // KZ == j)
        return jnp.minimum(k, KZ - 1), takes

    kappa, owning = owned(my)

    def count(s, total):
        col, k3 = wave_cols(wave_ref[:, slot(s)])
        return total + count_part(col, k3, kappa)

    counted = jnp.zeros((8, AT), f32)
    counted = lax.fori_loop(0, wave_ref.shape[1] // AT, count, counted, unroll=UNROLL)
    sigma, delta = weights(counted, kappa, lx, ly)
    left = radial_left(rad_ref[1, 0], rad_ref[1, 1])

    def frame_tile(t):
        for side, cell_at in enumerate(TILES[t]):
            if cell_at is not None:
                gfold[side * C : side * C + C, t * AT : (t + 1) * AT] = hfr[cell_at]

    mix_turned = [split2(mix_ref[1, p].T) for p in range(2)]
    cm_split, rh_turned = split2(cm_ref[...]), split2(rh_ref[...].T)
    gfold[C:, :AT] = jnp.zeros((C, AT), bf16)
    m_s[...] = jnp.zeros_like(m_s)
    passed = []
    for c, e in zip(along_y, (-1, 1)):
        c.wait_recv()
        passed.append(feature(4 - e, outer + 1 - e, 7 + e, cell(side, 0)))
        passed[-1].start()
    pending += passed
    for c in along_x:
        c.wait_recv()
    for t in range(3):
        frame_tile(t)

    def near_part(n, _):
        part_s[n] = dot(gfold[:, :NEAR], oht[:NEAR, slot(n)], NN)
        w_s[n] = dot(left, basis_right(basis_s[:, slot(n)]), NN)
        return 0

    lax.fori_loop(0, NB, near_part, 0, unroll=UNROLL)
    for e in (-1, 1):
        feature(4, outer + 1 + e, 1 + e, cell(0, e)).wait_recv()
        feature(4, inner + 1 + e, 1 + e, cell(0, e)).wait_recv()
    for t in range(3, 5):
        frame_tile(t)

    def forward(n, _):
        both = part_s[n] + dot(gfold[:, NEAR:], oht[NEAR:, slot(n)], NN)
        g = jnp.where(half_s[n] > 0, both[C:], both[:C])
        g_s[n] = g.astype(bf16)
        w = w_s[n]
        u = unit_s[:, slot(n)]
        m_s[0] += w[:C] * g
        t = w[C:] * g
        for p in range(3):
            m_s[1 + p] += t * u[p : p + 1]
        return 0

    lax.fori_loop(0, NB, forward, 0, unroll=UNROLL)
    m1 = [m_s[1 + p] * NORM for p in range(3)]
    sq = m1[0] * m1[0] + m1[1] * m1[1] + m1[2] * m1[2]
    act, slope2 = silu_pair(
        dot3s(mix_turned[0], m_s[0] * NORM) + dot3s(mix_turned[1], sq)
    )
    h2 = hfr[4].astype(f32) + act
    q = dot3s(cm_split, h2)
    for p in range(gx_n):
        q_send[p, :cq] = q[cq * p : cq * p + cq]
    q_recv[0, :cq] = q_send[mx, :cq]
    q_copies = {}
    for d in far_row:
        dev = cell(d, 0)
        q_copies[d] = remote(
            q_send.at[dev[0], :cq], q_recv.at[d, :cq], row_s.at[1, d], row_r.at[1, d], dev
        )
        q_copies[d].start()
    pending += q_copies.values()
    r, rs = silu_pair(dot3s(rh_turned, h2))
    ro8 = jnp.broadcast_to(ro_ref[...], (8, C))
    energy = dot3(ro8, r, NN)[0:1]
    dread = dot3(rh_ref[...] * ro_ref[...], rs, NN)

    t_s[...] = jnp.zeros_like(t_s)
    u_s[...] = jnp.zeros_like(u_s)
    near = [0] + far_row[::-1]
    for at in range(0, gx_n, UNROLL):
        for d in near[at : at + UNROLL]:
            if d:
                q_copies[d].wait_recv()
        for d in near[at : at + UNROLL]:
            q2 = jnp.concatenate([q_recv[d, :cq]] * 2, axis=0)
            main, rest = structure_cell(tr[d], q2, ph[d, 0:256], ph[d, 512:768], ph[d, 768:])
            t_s[...] += main
            u_s[...] += rest
    rows = 2 * cq
    rest = join_rest(u_s[...])
    for k in range(KZ):
        t_send[k, :, :256] = t_s[k * rows : (k + 1) * rows, :]
        t_send[k, :, 256:] = rest[k * rows : (k + 1) * rows]
    to_owner = []
    for d in far_col:
        dev = cell(0, d)
        k, takes = owned(dev[1])
        copy = remote(t_send.at[k], t_recv.at[my], red_s.at[d], red_r.at[my], dev)
        to_owner.append((takes, copy))
        pl.when(takes)(copy.start)

    spread = [
        remote(v_send, v_all.at[kappa], bc_s.at[d], bc_r.at[kappa], cell(0, d)) for d in far_col
    ]

    @pl.when(owning)
    def _():
        t_recv[my] = t_send[kappa]
        for d in range(1, gy_n):
            src = lax.rem(my + d, gy_n)
            remote(
                t_send.at[0], t_recv.at[src], red_s.at[1], red_r.at[src], (mx, src)
            ).wait_recv()
        total = t_recv[0]
        for j in range(1, gy_n):
            total = total + t_recv[j]
        v = weigh(total, sigma, delta)
        v_send[...] = v
        v_all[kappa] = v
        for c in spread:
            c.start()

    for k in range(KZ):
        arrive = remote(v_send, v_all.at[k], bc_s.at[0], bc_r.at[k], (mx, owners[k]))
        pl.when(my != owners[k])(arrive.wait_recv)

    v = jnp.concatenate([v_all[k] for k in range(KZ)], axis=0)
    lk[...] = fold_depth(fold_left(v, lx, ly))

    def back(d):
        dev = cell(-d, 0)
        return remote(
            b_send.at[d, : cq + 3], b_recv.at[mx, : cq + 3], row_s.at[2, d], row_r.at[2, d], dev
        )

    order = far_row + [0]
    for at in range(0, gx_n, UNROLL):
        for d in order[at : at + UNROLL]:
            b_send[d] = fold_cell(dot(lk[...], ph[d], NN), tr[d], q_recv[d, :cq])
        for d in order[at : at + UNROLL]:
            if d:
                back(d).start()
    b_recv[mx] = b_send[0]
    cm_turned = split2(cm_ref[...].T)
    mix_split = [split2(mix_ref[1, p]) for p in range(2)]
    rhi, rlo = split2(jnp.concatenate([rad_ref[1, 0], rad_ref[1, 1]], axis=1))
    rstack = jnp.concatenate([rhi.astype(f32), rlo.astype(f32)], axis=0).astype(bf16)
    for d in range(1, gx_n):
        src = lax.rem(mx + d, gx_n)
        remote(
            b_send.at[d, : cq + 3],
            b_recv.at[src, : cq + 3],
            row_s.at[2, d],
            row_r.at[2, d],
            (src, my),
        ).wait_recv()
    pot = jnp.concatenate([b_recv[p, :cq] for p in range(gx_n)], axis=0)
    long_range = b_recv[0, cq : cq + 3]
    for p in range(1, gx_n):
        long_range = long_range + b_recv[p, cq : cq + 3]
    site_ref[0] = energy + scale * colsum(q * pot)

    dh = dread + dot3s(cm_turned, pot * (2.0 * scale))
    dpre = dh * slope2
    d0 = dot3s(mix_split[0], dpre) * NORM
    dsq = dot3s(mix_split[1], dpre) * (2.0 * NORM)
    m_s[0] = d0
    for p in range(3):
        m_s[1 + p] = m1[p] * dsq

    def source_back(n, _):
        dgm = second_slot_source(
            w_s[n], half_s[n], unit_s[:, slot(n)], m_s[0], [m_s[1], m_s[2], m_s[3]]
        )
        dgm_s[:, slot(n)] = dgm.astype(bf16)
        return 0

    lax.fori_loop(0, NB, source_back, 0, unroll=UNROLL)

    def derivative(src, dst, sem_at, dev):
        return remote(g_send.at[src], g_recv.at[dst], halo_s.at[2, sem_at], halo_r.at[2, dst], dev)

    def spread_tile(t):
        return dot(dgm_s[...], oht[t * AT : (t + 1) * AT, :], NT)

    for t in (3, 4):
        part = spread_tile(t)
        g_send[TILES[t][0]] = part[:C].astype(bf16)
        g_send[TILES[t][1]] = part[C:].astype(bf16)
    shared = [derivative(inner + 1 + e, outer + 1 + e, 7 + e, cell(side, 0)) for e in (-1, 1)]
    corners = [derivative(outer + 1 + e, inner + 1 - e, 1 + e, cell(-side, e)) for e in (-1, 1)]
    for c in shared + corners:
        c.start()
    part = spread_tile(1)
    along_x = []
    for e, value in zip((-1, 1), (part[:C], part[C:])):
        g_send[4 + 3 * e] = value.astype(bf16)
        along_x.append(derivative(4 + 3 * e, 4 - 3 * e, 4 + 3 * e, cell(e, 0)))
        along_x[-1].start()
    part = spread_tile(2)
    along_y = []
    for e, value in zip((-1, 1), (part[:C], part[C:])):
        there = inner + 1 + e
        derivative(4, there, 7 + e, cell(side, 0)).wait_recv()
        g_send[4 + e] = (value + g_recv[there].astype(f32)).astype(bf16)
        along_y.append(derivative(4 + e, 4 - e, 4 + e, cell(0, e)))
        along_y[-1].start()
    pending += shared + corners + along_x + along_y
    grad = dh + spread_tile(0)[:C]

    def edge_back(n, _):
        u = unit_s[:, slot(n)]
        db, du = second_slot_back(
            g_s[n].astype(f32), w_s[n, C:], u, m_s[0], [m_s[1], m_s[2], m_s[3]], rhi, rstack
        )
        drel_s[:, slot(n)] = chain(db, du, slope_s[:, slot(n)], u, misc_s[0:1, slot(n)])
        return 0

    lax.fori_loop(0, NB, edge_back, 0, unroll=UNROLL)
    pairs = [pair_rows(rad_ref[0, p], embed8) for p in range(2)]
    straight = [split2(m) for m in pairs + [mix_ref[0, 0], mix_ref[0, 1]]]
    for c in along_x + along_y:
        c.wait_recv()
    for e in (-1, 1):
        derivative(4, outer + 1 + e, 1 + e, cell(0, e)).wait_recv()
        grad = grad + g_recv[outer + 1 + e].astype(f32)
        grad = grad + g_recv[4 + e].astype(f32) + g_recv[4 + 3 * e].astype(f32)

    sums = layer_one_back(grad, slope1, m1_first, *straight)
    own_grad = jnp.zeros((8, AT), f32)
    drels = []
    for n in range(NB):
        sl = slice(n * AT, (n + 1) * AT)
        b, u = basis_s[:, sl], unit_s[:, sl]
        db, du = first_sums_back(n, sums, b, u, misc_s[1:2, sl])
        drel = drel_s[:, sl] + chain(db, du, slope_s[:, sl], u, misc_s[0:1, sl])
        own_grad = own_grad - drel
        drels.append(drel)
    terms = [t.astype(f32) for t in split3(jnp.concatenate(drels, axis=1))]
    second = far > 0
    terms = [jnp.where(second, 0.0, t) for t in terms] + [
        jnp.where(second, t, 0.0) for t in terms
    ]
    terms = jnp.concatenate(terms, axis=0).astype(bf16)
    copies = []
    for t in (3, 4, 2, 1, 0):
        part = dot(terms, oht[t * AT : (t + 1) * AT, :], NT)
        low = part[:8] + part[8:16] + part[16:24]
        if t == 0:
            total = own_grad + low
            break
        for s, value in zip(TILES[t], (low, part[24:32] + part[32:40] + part[40:48])):
            f_send[s] = value
            copies += halo(
                3,
                lambda h: f_send.at[h, :3],
                lambda h: f_recv.at[h, :3],
                [(s // 3 - 1, s % 3 - 1)],
            )
    pending += copies
    total = total[:3]
    for c in copies:
        c.wait_recv()
    for s in range(9):
        if s != 4:
            total = total + f_recv[s, :3]
    total = total + (2.0 * scale) * long_range
    for p in range(3):
        force_ref[p] = -total[p : p + 1]

    for c in pending:
        c.wait_send()
    for takes, copy in to_owner:
        pl.when(takes)(copy.wait_send)

    @pl.when(owning)
    def _():
        for c in spread:
            c.wait_send()

    for d in range(1, gx_n):
        back(d).wait_send()


def per_device(
    positions,
    species,
    neighbours,
    counts,
    species_embed,
    radial,
    mixing,
    read_hidden,
    read_out,
    charge_map,
    wavevectors,
):
    gx_n, gy_n = lax.axis_size("gx"), lax.axis_size("gy")
    rows = 2 * (charge_map.shape[1] // gx_n)
    vmem = pltpu.VMEM
    sem = pltpu.SemaphoreType.DMA
    scratch = [
        vmem((9, 8, AT), f32),
        vmem((gx_n, 8, AT), f32),
        vmem((9, C, AT), bf16),
        vmem((HALF, E), bf16),
        vmem((NB, 1, AT), jnp.int32),
        vmem((NB, 1, AT), jnp.int32),
        vmem((NB, 2 * C, AT), f32),
        vmem((48, E), f32),
        vmem((2 * C, HALF), bf16),
        vmem((NB, C, AT), bf16),
        vmem((NB, 2 * C, AT), f32),
        vmem((2 * C, E), bf16),
        vmem((8, E), f32),
        vmem((8, E), f32),
        vmem((8, E), f32),
        vmem((8, E), f32),
        vmem((8, E), f32),
        vmem((4, C, AT), f32),
        vmem((gx_n, DEPTH, AT), bf16),
        vmem((gx_n, KZ * rows, AT), f32),
        vmem((KZ * rows, 256), f32),
        vmem((2 * KZ * rows, 128), f32),
        vmem((3 * KZ * rows, DEPTH), bf16),
        vmem((gx_n, rows, AT), f32),
        vmem((gx_n, rows, AT), f32),
        vmem((KZ, rows, LANES), f32),
        vmem((gy_n, rows, LANES), f32),
        vmem((rows, LANES), f32),
        vmem((KZ, rows, LANES), f32),
        vmem((gx_n, 8, AT), f32),
        vmem((gx_n, 8, AT), f32),
        vmem((9, C, AT), bf16),
        vmem((9, C, AT), bf16),
        vmem((9, 8, AT), f32),
        vmem((9, 8, AT), f32),
        sem((4, 9)),
        sem((4, 9)),
        sem((3, gx_n)),
        sem((3, gx_n)),
        sem((gy_n,)),
        sem((gy_n,)),
        sem((gy_n,)),
        sem((KZ,)),
    ]
    arrays = (
        jnp.transpose(positions[0], (1, 0, 2)),
        species,
        jnp.transpose(neighbours[0], (2, 0, 1)),
        counts,
        species_embed,
        radial,
        mixing,
        read_hidden,
        read_out[None],
        charge_map.T,
        wavevectors,
    )
    forces, site_energy = pl.pallas_call(
        functools.partial(kernel, gx_n, gy_n),
        out_shape=(
            jax.ShapeDtypeStruct((3, 1, AT), f32),
            jax.ShapeDtypeStruct((1, 1, AT), f32),
        ),
        in_specs=[pl.BlockSpec(memory_space=pl.ANY)] * len(arrays),
        out_specs=(pl.BlockSpec(memory_space=pltpu.VMEM),) * 2,
        scratch_shapes=[vmem(a.shape, a.dtype) for a in arrays] + [sem((len(arrays),))] + scratch,
        compiler_params=pltpu.CompilerParams(
            collective_id=0, has_side_effects=True, vmem_limit_bytes=60 * 1024 * 1024
        ),
    )(*arrays)
    return jnp.transpose(forces, (1, 0, 2))[None], site_energy


def solution(mesh):
    in_specs = (
        P("gx", "gy", None, None),
        P("gx", "gy", None),
        P("gx", "gy", None, None),
        P("gx", "gy", None),
        P(),
        P(),
        P(),
        P(),
        P(),
        P(),
        P(),
    )
    out_specs = (P("gx", "gy", None, None), P("gx", "gy", None))
    return jax.shard_map(
        per_device, mesh=mesh, in_specs=in_specs, out_specs=out_specs, check_vma=False
    )
```

```python
import functools
import math

import jax
import jax.numpy as jnp
from jax import lax
from jax.experimental import pallas as pl
from jax.experimental.pallas import tpu as pltpu
from jax.sharding import PartitionSpec as P

MESH = pl.DeviceIdType.MESH
f32, bf16 = jnp.float32, jnp.bfloat16
NN, NT, TN = ((1,), (0,)), ((1,), (1,)), ((0,), (0,))
CELL, HEIGHT, CUT = 10.0, 30.0, 50.0
AT, NB, C, NR, NS = 256, 12, 128, 8, 6
E = AT * NB
HALF = 1280
KZ = 9
LANES = 384
DEPTH = 896
UNROLL = 4
NORM = 1.0 / math.sqrt(NB)
TILES = ((4, None), (1, 7), (3, 5), (0, 2), (6, 8))
NEAR = 3 * AT


def dot(a, b, dims):
    return lax.dot_general(a, b, (dims, ((), ())), preferred_element_type=f32)


def split2(x):
    hi = x.astype(bf16)
    return hi, (x - hi.astype(f32)).astype(bf16)


def split3(x):
    hi = x.astype(bf16)
    rest = x - hi.astype(f32)
    mid = rest.astype(bf16)
    return hi, mid, (rest - mid.astype(f32)).astype(bf16)


def dot3(a, b, dims):
    ah, al = split2(a)
    bh, bl = split2(b)
    return dot(ah, bh, dims) + dot(ah, bl, dims) + dot(al, bh, dims)


def dot3s(a, b):
    bh, bl = split2(b)
    return dot(a[0], bh, NN) + dot(a[0], bl, NN) + dot(a[1], bh, NN)


def rowid(shape):
    return lax.broadcasted_iota(jnp.int32, shape, 0)


def laneid(shape):
    return lax.broadcasted_iota(jnp.int32, shape, 1)


def sigmoid(x):
    return 1.0 / (1.0 + jnp.exp(-x))


def silu_pair(x):
    s = sigmoid(x)
    return x * s, s * (1.0 + x * (1.0 - s))


def swap_rows(x):
    h = x.shape[0] // 2
    return jnp.concatenate([x[h:], x[:h]], axis=0)


def shift_lanes(x, by):
    by = by % x.shape[1]
    return jnp.concatenate([x[:, -by:], x[:, :-by]], axis=1)


def swap_sixteens(x):
    return jnp.where(laneid(x.shape) < 16, shift_lanes(x, -16), shift_lanes(x, 16))


def colsum(x):
    return jnp.sum(x, axis=0, keepdims=True)


def folded(idx_row):
    which = idx_row >> 8
    tile, far = jnp.zeros_like(idx_row), jnp.zeros_like(idx_row)
    for t, pair in enumerate(TILES[1:], 1):
        tile = jnp.where((which == pair[0]) | (which == pair[1]), t, tile)
        far = jnp.where(which == pair[1], 1, far)
    return tile * AT + (idx_row & (AT - 1)), far


def one_hot(f):
    return jnp.where(rowid((HALF, AT)) == f, 1.0, 0.0).astype(bf16)


def pos_table(frame, tiles):
    parts = []
    for side in range(2):
        cells = []
        for pair in tiles:
            s = pair[side]
            if s is None:
                cells.append(jnp.zeros((8, AT), f32))
                continue
            a, b = divmod(s, 3)
            r = rowid((8, AT))
            shift = jnp.where(r == 0, CELL * (a - 1), 0.0) + jnp.where(r == 1, CELL * (b - 1), 0.0)
            cells.append(frame[s] + shift)
        parts += [t.astype(f32) for t in split3(jnp.concatenate(cells, axis=1))]
    return jnp.concatenate(parts, axis=0).astype(bf16)


def geometry(gathered, far, own, cnt):
    low = gathered[0:8] + gathered[8:16] + gathered[16:24]
    high = gathered[24:32] + gathered[32:40] + gathered[40:48]
    pos = jnp.where(far > 0, high, low)
    rel = jnp.where(rowid((8, E)) < 3, pos - jnp.concatenate([own] * NB, axis=1), 0.0)
    kind = pos[3:4]
    dist = jnp.sqrt(colsum(rel * rel) + 0.25)
    inv = 1.0 / dist
    unit = rel * inv
    freq = (rowid((8, 1)) + 1).astype(f32) * (math.pi / CUT)
    arg = dist * freq
    live = jnp.concatenate([jnp.where(n < cnt, 1.0, 0.0) for n in range(NB)], axis=1)
    basis = jnp.sin(arg) / arg
    slope = (jnp.cos(arg) - basis) * (inv * live)
    return basis * live, slope, unit, inv, kind


def chain(db, du, slope, unit, inv):
    return du * inv + unit * (colsum(db * slope) - inv * colsum(du * unit))


def kind_rows(kind):
    return jnp.where(rowid((8, AT)).astype(f32) == kind, 1.0, 0.0).astype(bf16)


def embed_cols(embed8, kind):
    oh = kind_rows(kind)
    hi, mid, lo = split3(embed8)
    return dot(hi, oh, TN) + dot(mid, oh, TN) + dot(lo, oh, TN)


def first_sums(basis, unit, kind):
    sums = [jnp.zeros((32, AT), f32) for _ in range(NS)]
    for n in range(NB):
        sl = slice(n * AT, (n + 1) * AT)
        b, u, k = basis[:, sl], unit[:, sl], kind[:, sl]
        z = jnp.concatenate([b, b * u[0:1], b * u[1:2], b * u[2:3]], axis=0)
        for s in range(NS):
            sums[s] = sums[s] + jnp.where(k == float(s), z, 0.0)
    return [jnp.concatenate([t[8 * p : 8 * p + 8] for t in sums], axis=0) for p in range(4)]


def pair_rows(radial, embed8):
    return jnp.concatenate([radial * embed8[s : s + 1] for s in range(NS)], axis=0)


def layer_one(sums, initial, re0, re1, mix0, mix1):
    m0 = dot3s(re0, sums[0]) * NORM
    m1 = dot3s(re1, jnp.concatenate(sums[1:], axis=1)) * NORM
    mx = [m1[:, p * AT : (p + 1) * AT] for p in range(3)]
    sq = mx[0] * mx[0] + mx[1] * mx[1] + mx[2] * mx[2]
    act, slope = silu_pair(dot3s(mix0, m0) + dot3s(mix1, sq))
    return initial + act, slope, m1


def layer_one_back(grad, slope, m1, re0, re1, mix0, mix1):
    dpre = grad * slope
    d0 = dot3s(mix0, dpre) * NORM
    dsq = dot3s(mix1, dpre) * (2.0 * NORM)
    d1 = m1 * jnp.concatenate([dsq] * 3, axis=1)
    a0 = dot3s(re0, d0)
    a1 = dot3s(re1, d1)
    return [a0] + [a1[:, p * AT : (p + 1) * AT] for p in range(3)]


def first_sums_back(n, sums, basis, unit, kind):
    z = []
    for t in sums:
        got = jnp.zeros((8, AT), f32)
        for s in range(NS):
            got = jnp.where(kind == float(s), t[8 * s : 8 * s + 8], got)
        z.append(got)
    db = z[0] + z[1] * unit[0:1] + z[2] * unit[1:2] + z[3] * unit[2:3]
    du = [colsum(basis * t) for t in z[1:]]
    return db, jnp.concatenate(du + [jnp.zeros((5, AT), f32)], axis=0)


def radial_left(radial0, radial1):
    r = jnp.concatenate([radial0, radial1], axis=1)
    hi, lo = split2(r)
    hi, lo = hi.astype(f32), lo.astype(f32)
    return jnp.concatenate([hi, hi, lo, jnp.zeros_like(hi)], axis=0).T.astype(bf16)


def basis_right(b):
    hi, lo = split2(b)
    hi, lo = hi.astype(f32), lo.astype(f32)
    return jnp.concatenate([hi, lo, hi, jnp.zeros_like(hi)], axis=0).astype(bf16)


def second_slot_source(w, far, unit, d0, d1):
    p = d1[0] * unit[0:1] + d1[1] * unit[1:2] + d1[2] * unit[2:3]
    dg = w[:C] * d0 + w[C:] * p
    far = far > 0
    return jnp.concatenate([jnp.where(far, 0.0, dg), jnp.where(far, dg, 0.0)], axis=0)


def second_slot_back(g, w1, unit, d0, d1, rhi, rstack):
    p = d1[0] * unit[0:1] + d1[1] * unit[1:2] + d1[2] * unit[2:3]
    xh, xl = split2(jnp.concatenate([g * d0, g * p], axis=0))
    both = dot(rstack, xh, NN)
    db = both[:8] + both[8:] + dot(rhi, xl, NN)
    t = w1 * g
    du = [colsum(t * d) for d in d1]
    return db, jnp.concatenate(du + [jnp.zeros((5, AT), f32)], axis=0)


def trig8(pos_row, origin, length):
    theta = (pos_row + origin) * (2.0 * math.pi / length)
    arg = theta * (rowid((8, 1)) + 1).astype(f32)
    return jnp.cos(arg), jnp.sin(arg)


def phases(pos, ox, oy, lx, ly, cq):
    c1, s1 = trig8(pos[0:1], ox, lx)
    c2, s2 = trig8(pos[1:2], oy, ly)
    c3, s3 = trig8(pos[2:3], 0.0, HEIGHT)
    cos, sin = [], []
    for m in range(8):
        a, b = c1[m : m + 1], s1[m : m + 1]
        cc, ss, sc, cs = a * c2, b * s2, b * c2, a * s2
        cos += [cc - ss, cc + ss]
        sin += [sc + cs, sc - cs]
    main = jnp.concatenate(cos + sin, axis=0)
    rest = jnp.concatenate([c1, c2, s1, s2], axis=0)
    third = [jnp.where(rowid((2 * cq, AT)) < cq, 1.0, 0.0)]
    for m in range(8):
        third.append(jnp.where(rowid((2 * cq, AT)) < cq, c3[m : m + 1], s3[m : m + 1]))
    return main, rest, jnp.concatenate(third, axis=0)


def phase_rows(main, rest):
    mh, ml = split2(main)
    rh, rl = (t.astype(f32) for t in split2(rest))
    tail = jnp.concatenate([rh, rh, rl, jnp.zeros_like(rh)], axis=0).astype(bf16)
    return mh, ml, tail


def structure_cell(third, q2, mh, ml, tail):
    n = third.shape[0]
    qh, ql = split2(third * jnp.concatenate([q2] * KZ, axis=0))
    qq = jnp.concatenate([qh, ql], axis=0)
    both = dot(qq, mh, NT)
    return both[:n] + both[n:] + dot(qh, ml, NT), dot(qq, tail, NT)


def join_rest(both):
    n = both.shape[0] // 2
    return both[:n] + both[n:] + shift_lanes(both[:n], -64)


def fold_depth(left):
    hi, lo = split2(left)
    rh, rl = hi[:, 256:].astype(f32), lo[:, 256:].astype(f32)
    tail = (rh + shift_lanes(rl, 32) + shift_lanes(rh, 64)).astype(bf16)
    return jnp.concatenate([hi[:, :256], lo[:, :256], hi[:, :256], tail], axis=1)


def wave_cols(waves):
    k1, k2, k3 = waves[0:1], waves[1:2], waves[2:3]
    flip = (k1 < 0) | ((k1 == 0) & (k2 < 0))
    k1, k2, k3 = (jnp.where(flip, -k, k) for k in (k1, k2, k3))
    main = (k1 - 1) * 16 + jnp.where(k2 > 0, k2 - 1, 7 - k2)
    col = jnp.where(k1 == 0, 135 + k2, jnp.where(k2 == 0, 127 + k1, main))
    return col, k3


def count_part(col, k3, kappa):
    oh = jnp.where(rowid((256, AT)) == col, 1.0, 0.0).astype(bf16)
    r = rowid((8, AT))
    want = jnp.where(r == 0, kappa, jnp.where(r == 1, -kappa, 99))
    return dot(jnp.where(k3 == want, 1.0, 0.0).astype(bf16), oh, NT)


def col_numbers():
    lane = laneid((1, 256))
    low = (lane & 7) + 1
    k1 = jnp.where(lane < 128, (lane >> 4) + 1, jnp.where(lane < 136, low, 0))
    k2 = jnp.where(lane < 128, jnp.where((lane & 15) < 8, low, -low), jnp.where(lane < 136, 0, low))
    k1, k2 = jnp.where(lane < 144, k1, 0), jnp.where(lane < 144, k2, 0)
    return k1.astype(f32), k2.astype(f32)


def widen(x):
    main, rest = x[:, :128], x[:, 128:]
    rest = rest + shift_lanes(rest, 16)
    return jnp.concatenate([main, main, rest], axis=1)


def weights(count, kappa, lx, ly):
    k1, k2 = col_numbers()
    kz = kappa.astype(f32)
    wx, wy, wz = 2.0 * math.pi * k1 / lx, 2.0 * math.pi * k2 / ly, 2.0 * math.pi * kz / HEIGHT
    sq = wx * wx + wy * wy + wz * wz
    green = jnp.exp(-0.5 * sq) / (sq + 0.25)
    plus = count[0:1] * green
    minus = jnp.where(kappa == 0, 0.0, count[1:2] * green)
    return widen(plus + minus), widen(plus - minus)


def turn(t, sign):
    rest = t[:, 256:]
    swapped = swap_sixteens(rest)
    rest = jnp.where(laneid(rest.shape) < 16, sign * swapped, -sign * swapped)
    return jnp.concatenate([sign * t[:, 128:256], -sign * t[:, :128], rest], axis=1)


def weigh(t, sigma, delta):
    cq = t.shape[0] // 2
    sign = jnp.where(rowid((2 * cq, 1)) < cq, -1.0, 1.0)
    return sigma * t + delta * turn(swap_rows(t), sign)


def fold_left(v, lx, ly):
    k1, k2 = col_numbers()
    kx, ky = widen(k1) * (2.0 * math.pi / lx), widen(k2) * (2.0 * math.pi / ly)
    t = turn(v, 1.0)
    return jnp.concatenate([v, kx * t, ky * t], axis=0)


def fold_cell(u, third, q):
    cq = q.shape[0]
    rows = KZ * 2 * cq
    zero = jnp.zeros((2 * cq, AT), f32)
    pot, gx, gy, gz = zero, zero, zero, zero
    for k in range(KZ):
        at = slice(k * 2 * cq, (k + 1) * 2 * cq)
        t, part = third[at], u[at]
        pot = pot + t * part
        gx = gx + t * u[rows:][at]
        gy = gy + t * u[2 * rows :][at]
        if k:
            gz = gz + swap_rows(t) * (part * (2.0 * math.pi * k / HEIGHT))
    qq = jnp.concatenate([q, q], axis=0)
    sign = jnp.where(rowid((2 * cq, 1)) < cq, -1.0, 1.0)
    rows = [pot[:cq] + pot[cq:], colsum(qq * gx), colsum(qq * gy), colsum(qq * gz * sign)]
    return jnp.concatenate(rows + [jnp.zeros((1, AT), f32)], axis=0)


def kernel(
    gx_n,
    gy_n,
    *refs,
):
    arrays, (force_ref, site_ref), rest = refs[:11], refs[11:13], refs[13:]
    kept, load_s, rest = rest[:11], rest[11], rest[12:]
    pos_ref, kind_ref, nbr_ref, cnt_ref, emb_ref, rad_ref, mix_ref, rh_ref = kept[:8]
    ro_ref, cm_ref, wave_ref = kept[8:]
    (
        pfr, prow, hfr, oht, half_s, fold_s, part_s, gp_s, gfold, g_s, w_s, dgm_s,
        drel_s, basis_s, slope_s, unit_s, misc_s, m_s, ph, tr, t_s, u_s, lk, q_send,
        q_recv, t_send, t_recv, v_send, v_all, b_send, b_recv, g_send, g_recv, f_send,
        f_recv, halo_s, halo_r, row_s, row_r, red_s, red_r, bc_s, bc_r,
    ) = rest
    mx, my = lax.axis_index("gx"), lax.axis_index("gy")
    cq = cm_ref.shape[0] // gx_n
    lx, ly = CELL * gx_n, CELL * gy_n
    atoms_all = AT * gx_n * gy_n
    scale = 1.0 / math.sqrt(wave_ref.shape[1] * cm_ref.shape[0] * atoms_all)

    def cell(da, db):
        return lax.rem(mx + da + gx_n, gx_n), lax.rem(my + db + gy_n, gy_n)

    around = [(da, db) for da in (-1, 0, 1) for db in (-1, 0, 1) if (da, db) != (0, 0)]
    around.sort(key=lambda t: -abs(t[0]) - abs(t[1]))
    far_col = sorted(range(1, gy_n), key=lambda d: -min(d % 4, 4 - d % 4) - min(d // 4, 4 - d // 4))
    far_row = sorted(range(1, gx_n), key=lambda d: -min(d, gx_n - d))

    def remote(src, dst, ssem, rsem, dev):
        return pltpu.make_async_remote_copy(
            src_ref=src,
            dst_ref=dst,
            send_sem=ssem,
            recv_sem=rsem,
            device_id=dev,
            device_id_type=MESH,
        )

    def halo(stage, src_of, dst_of, pick=None):
        copies = []
        for da, db in around if pick is None else pick:
            here, there = 3 * (da + 1) + db + 1, 3 * (1 - da) + 1 - db
            copies.append(
                remote(
                    src_of(here),
                    dst_of(there),
                    halo_s.at[stage, here],
                    halo_r.at[stage, there],
                    cell(da, db),
                )
            )
            copies[-1].start()
        return copies

    pending = []
    pfr[...] = jnp.zeros_like(pfr)
    loads = [
        pltpu.make_async_copy(a, k, load_s.at[i]) for i, (a, k) in enumerate(zip(arrays, kept))
    ]

    barrier = pltpu.get_barrier_semaphore()
    mates = [cell(d, 0) for d in range(1, gx_n)] + [cell(0, d) for d in range(1, gy_n)]
    mates += [cell(da, db) for da, db in around if da and db]
    for dev in mates:
        pl.semaphore_signal(barrier, inc=1, device_id=dev, device_id_type=MESH)

    for c in loads:
        c.start()
    for c in loads[:2]:
        c.wait()
    row = rowid((8, AT))
    own = jnp.where(row == 3, kind_ref[0].astype(f32), 0.0)
    for p in range(3):
        own = jnp.where(row == p, pos_ref[p], own)
    pfr[4] = own
    prow[0] = own
    pl.semaphore_wait(barrier, len(mates))

    copies = halo(0, lambda here: pfr.at[4, :4], lambda there: pfr.at[there, :4])
    row_pos = [
        remote(prow.at[0, :3], prow.at[d, :3], row_s.at[0, d], row_r.at[0, d], cell(d, 0))
        for d in far_row
    ]
    for c in row_pos:
        c.start()
    pending += copies + row_pos
    for c in loads[2:]:
        c.wait()

    def slot(n):
        return pl.ds(pl.multiple_of(n * AT, AT), AT)

    def hot(n, _):
        f, far = folded(nbr_ref[n])
        fold_s[n] = f
        half_s[n] = far
        oht[:, slot(n)] = one_hot(f)
        return 0

    lax.fori_loop(0, NB, hot, 0)
    embed8 = jnp.zeros((8, C), f32)
    for s in range(NS):
        embed8 = jnp.where(rowid((8, C)) == s, emb_ref[s : s + 1, :], embed8)
    far = jnp.concatenate([half_s[n] for n in range(NB)], axis=1)
    initial = embed_cols(embed8, own[3:4])
    pairs = [pair_rows(rad_ref[0, p], embed8) for p in range(2)]
    turned = [split2(m.T) for m in pairs + [mix_ref[0, 0], mix_ref[0, 1]]]
    for c in copies[4:]:
        c.wait_recv()
    gp_s[...] = dot(pos_table(pfr, TILES[:3]), oht[:NEAR, :], NN)
    for c in copies[:4]:
        c.wait_recv()

    gathered = gp_s[...] + dot(pos_table(pfr, TILES[3:]), oht[NEAR:, :], NN)
    basis, slope, unit, inv, kind = geometry(gathered, far, own, cnt_ref[0])
    basis_s[...] = basis
    slope_s[...] = slope
    unit_s[...] = unit
    misc_s[0:1] = inv
    misc_s[1:2] = kind
    hidden, slope1, m1_first = layer_one(first_sums(basis, unit, kind), initial, *turned)
    hfr[4] = hidden.astype(bf16)
    side = 1 - 2 * lax.rem(mx, 2)
    outer, inner = 3 * (1 - side), 3 * (1 + side)

    def feature(src, dst, sem_at, dev):
        return remote(hfr.at[src], hfr.at[dst], halo_s.at[1, sem_at], halo_r.at[1, dst], dev)

    along_y = [feature(4, 4 - e, 4 + e, cell(0, e)) for e in (-1, 1)]
    corners = [feature(4, inner + 1 - e, 1 + e, cell(-side, e)) for e in (-1, 1)]
    along_x = [feature(4, 4 - 3 * e, 4 + 3 * e, cell(e, 0)) for e in (-1, 1)]
    for c in along_y + corners + along_x:
        c.start()
    pending += along_y + corners + along_x

    for c in row_pos:
        c.wait_recv()

    def phase(d, _):
        source = lax.rem(mx - d + gx_n, gx_n)
        main, rest, third = phases(
            prow[d], source.astype(f32) * CELL, my.astype(f32) * CELL, lx, ly, cq
        )
        mh, ml, tail = phase_rows(main, rest)
        ph[d, 0:256] = mh
        ph[d, 256:512] = mh
        ph[d, 512:768] = ml
        ph[d, 768:] = tail
        tr[d] = third
        return 0

    lax.fori_loop(0, gx_n, phase, 0, unroll=UNROLL)
    owners = [k * gy_n // KZ for k in range(KZ)]

    def owned(j):
        k = (j * KZ + gy_n - 1) // gy_n
        takes = (k < KZ) & ((k * gy_n) // KZ == j)
        return jnp.minimum(k, KZ - 1), takes

    kappa, owning = owned(my)

    def count(s, total):
        col, k3 = wave_cols(wave_ref[:, slot(s)])
        return total + count_part(col, k3, kappa)

    counted = jnp.zeros((8, AT), f32)
    counted = lax.fori_loop(0, wave_ref.shape[1] // AT, count, counted, unroll=UNROLL)
    sigma, delta = weights(counted, kappa, lx, ly)
    left = radial_left(rad_ref[1, 0], rad_ref[1, 1])

    def frame_tile(t):
        for side, cell_at in enumerate(TILES[t]):
            if cell_at is not None:
                gfold[side * C : side * C + C, t * AT : (t + 1) * AT] = hfr[cell_at]

    mix_turned = [split2(mix_ref[1, p].T) for p in range(2)]
    cm_split, rh_turned = split2(cm_ref[...]), split2(rh_ref[...].T)
    gfold[C:, :AT] = jnp.zeros((C, AT), bf16)
    m_s[...] = jnp.zeros_like(m_s)
    def radial_part(n, _):
        w_s[n] = dot(left, basis_right(basis_s[:, slot(n)]), NN)
        return 0

    lax.fori_loop(0, NB, radial_part, 0, unroll=UNROLL)
    passed = []
    for c, e in zip(along_y, (-1, 1)):
        c.wait_recv()
        passed.append(feature(4 - e, outer + 1 - e, 7 + e, cell(side, 0)))
        passed[-1].start()
    pending += passed
    for c in along_x:
        c.wait_recv()
    for t in range(3):
        frame_tile(t)

    def near_part(n, _):
        part_s[n] = dot(gfold[:, :NEAR], oht[:NEAR, slot(n)], NN)
        return 0

    lax.fori_loop(0, NB, near_part, 0, unroll=UNROLL)
    for e in (-1, 1):
        feature(4, outer + 1 + e, 1 + e, cell(0, e)).wait_recv()
        feature(4, inner + 1 + e, 1 + e, cell(0, e)).wait_recv()
    for t in range(3, 5):
        frame_tile(t)

    def forward(n, _):
        both = part_s[n] + dot(gfold[:, NEAR:], oht[NEAR:, slot(n)], NN)
        g = jnp.where(half_s[n] > 0, both[C:], both[:C])
        g_s[n] = g.astype(bf16)
        w = w_s[n]
        u = unit_s[:, slot(n)]
        m_s[0] += w[:C] * g
        t = w[C:] * g
        for p in range(3):
            m_s[1 + p] += t * u[p : p + 1]
        return 0

    lax.fori_loop(0, NB, forward, 0, unroll=6)
    m1 = [m_s[1 + p] * NORM for p in range(3)]
    sq = m1[0] * m1[0] + m1[1] * m1[1] + m1[2] * m1[2]
    act, slope2 = silu_pair(
        dot3s(mix_turned[0], m_s[0] * NORM) + dot3s(mix_turned[1], sq)
    )
    h2 = hfr[4].astype(f32) + act
    q = dot3s(cm_split, h2)
    for p in range(gx_n):
        q_send[p, :cq] = q[cq * p : cq * p + cq]
    q_recv[0, :cq] = q_send[mx, :cq]
    q_copies = {}
    for d in far_row:
        dev = cell(d, 0)
        q_copies[d] = remote(
            q_send.at[dev[0], :cq], q_recv.at[d, :cq], row_s.at[1, d], row_r.at[1, d], dev
        )
        q_copies[d].start()
    pending += q_copies.values()
    r, rs = silu_pair(dot3s(rh_turned, h2))
    ro8 = jnp.broadcast_to(ro_ref[...], (8, C))
    energy = dot3(ro8, r, NN)[0:1]
    dread = dot3(rh_ref[...] * ro_ref[...], rs, NN)

    t_s[...] = jnp.zeros_like(t_s)
    u_s[...] = jnp.zeros_like(u_s)
    near = [0] + far_row[::-1]
    for at in range(0, gx_n, UNROLL):
        for d in near[at : at + UNROLL]:
            if d:
                q_copies[d].wait_recv()
        for d in near[at : at + UNROLL]:
            q2 = jnp.concatenate([q_recv[d, :cq]] * 2, axis=0)
            main, rest = structure_cell(tr[d], q2, ph[d, 0:256], ph[d, 512:768], ph[d, 768:])
            t_s[...] += main
            u_s[...] += rest
    rows = 2 * cq
    rest = join_rest(u_s[...])
    for k in range(KZ):
        t_send[k, :, :256] = t_s[k * rows : (k + 1) * rows, :]
        t_send[k, :, 256:] = rest[k * rows : (k + 1) * rows]
    to_owner = []
    for d in far_col:
        dev = cell(0, d)
        k, takes = owned(dev[1])
        copy = remote(t_send.at[k], t_recv.at[my], red_s.at[d], red_r.at[my], dev)
        to_owner.append((takes, copy))
        pl.when(takes)(copy.start)

    spread = [
        remote(v_send, v_all.at[kappa], bc_s.at[d], bc_r.at[kappa], cell(0, d)) for d in far_col
    ]

    @pl.when(owning)
    def _():
        t_recv[my] = t_send[kappa]
        for d in range(1, gy_n):
            src = lax.rem(my + d, gy_n)
            remote(
                t_send.at[0], t_recv.at[src], red_s.at[1], red_r.at[src], (mx, src)
            ).wait_recv()
        total = t_recv[0]
        for j in range(1, gy_n):
            total = total + t_recv[j]
        v = weigh(total, sigma, delta)
        v_send[...] = v
        v_all[kappa] = v
        for c in spread:
            c.start()

    for k in range(KZ):
        arrive = remote(v_send, v_all.at[k], bc_s.at[0], bc_r.at[k], (mx, owners[k]))
        pl.when(my != owners[k])(arrive.wait_recv)

    v = jnp.concatenate([v_all[k] for k in range(KZ)], axis=0)
    lk[...] = fold_depth(fold_left(v, lx, ly))

    def back(d):
        dev = cell(-d, 0)
        return remote(
            b_send.at[d, : cq + 3], b_recv.at[mx, : cq + 3], row_s.at[2, d], row_r.at[2, d], dev
        )

    order = far_row + [0]
    for at in range(0, gx_n, UNROLL):
        for d in order[at : at + UNROLL]:
            b_send[d] = fold_cell(dot(lk[...], ph[d], NN), tr[d], q_recv[d, :cq])
        for d in order[at : at + UNROLL]:
            if d:
                back(d).start()
    b_recv[mx] = b_send[0]
    cm_turned = split2(cm_ref[...].T)
    mix_split = [split2(mix_ref[1, p]) for p in range(2)]
    rhi, rlo = split2(jnp.concatenate([rad_ref[1, 0], rad_ref[1, 1]], axis=1))
    rstack = jnp.concatenate([rhi.astype(f32), rlo.astype(f32)], axis=0).astype(bf16)
    for d in range(1, gx_n):
        src = lax.rem(mx + d, gx_n)
        remote(
            b_send.at[d, : cq + 3],
            b_recv.at[src, : cq + 3],
            row_s.at[2, d],
            row_r.at[2, d],
            (src, my),
        ).wait_recv()
    pot = jnp.concatenate([b_recv[p, :cq] for p in range(gx_n)], axis=0)
    long_range = b_recv[0, cq : cq + 3]
    for p in range(1, gx_n):
        long_range = long_range + b_recv[p, cq : cq + 3]
    site_ref[0] = energy + scale * colsum(q * pot)

    dh = dread + dot3s(cm_turned, pot * (2.0 * scale))
    dpre = dh * slope2
    d0 = dot3s(mix_split[0], dpre) * NORM
    dsq = dot3s(mix_split[1], dpre) * (2.0 * NORM)
    m_s[0] = d0
    for p in range(3):
        m_s[1 + p] = m1[p] * dsq

    def source_back(n, _):
        dgm = second_slot_source(
            w_s[n], half_s[n], unit_s[:, slot(n)], m_s[0], [m_s[1], m_s[2], m_s[3]]
        )
        dgm_s[:, slot(n)] = dgm.astype(bf16)
        return 0

    lax.fori_loop(0, NB, source_back, 0, unroll=UNROLL)

    def derivative(src, dst, sem_at, dev):
        return remote(g_send.at[src], g_recv.at[dst], halo_s.at[2, sem_at], halo_r.at[2, dst], dev)

    def spread_tile(t):
        return dot(dgm_s[...], oht[t * AT : (t + 1) * AT, :], NT)

    for t in (3, 4):
        part = spread_tile(t)
        g_send[TILES[t][0]] = part[:C].astype(bf16)
        g_send[TILES[t][1]] = part[C:].astype(bf16)
    shared = [derivative(inner + 1 + e, outer + 1 + e, 7 + e, cell(side, 0)) for e in (-1, 1)]
    corners = [derivative(outer + 1 + e, inner + 1 - e, 1 + e, cell(-side, e)) for e in (-1, 1)]
    for c in shared + corners:
        c.start()
    part = spread_tile(1)
    along_x = []
    for e, value in zip((-1, 1), (part[:C], part[C:])):
        g_send[4 + 3 * e] = value.astype(bf16)
        along_x.append(derivative(4 + 3 * e, 4 - 3 * e, 4 + 3 * e, cell(e, 0)))
        along_x[-1].start()
    part = spread_tile(2)
    along_y = []
    for e, value in zip((-1, 1), (part[:C], part[C:])):
        there = inner + 1 + e
        derivative(4, there, 7 + e, cell(side, 0)).wait_recv()
        g_send[4 + e] = (value + g_recv[there].astype(f32)).astype(bf16)
        along_y.append(derivative(4 + e, 4 - e, 4 + e, cell(0, e)))
        along_y[-1].start()
    pending += shared + corners + along_x + along_y
    grad = dh + spread_tile(0)[:C]

    def edge_back(n, _):
        u = unit_s[:, slot(n)]
        db, du = second_slot_back(
            g_s[n].astype(f32), w_s[n, C:], u, m_s[0], [m_s[1], m_s[2], m_s[3]], rhi, rstack
        )
        drel_s[:, slot(n)] = chain(db, du, slope_s[:, slot(n)], u, misc_s[0:1, slot(n)])
        return 0

    lax.fori_loop(0, NB, edge_back, 0, unroll=UNROLL)
    pairs = [pair_rows(rad_ref[0, p], embed8) for p in range(2)]
    straight = [split2(m) for m in pairs + [mix_ref[0, 0], mix_ref[0, 1]]]
    for c in along_x + along_y:
        c.wait_recv()
    for e in (-1, 1):
        derivative(4, outer + 1 + e, 1 + e, cell(0, e)).wait_recv()
        grad = grad + g_recv[outer + 1 + e].astype(f32)
        grad = grad + g_recv[4 + e].astype(f32) + g_recv[4 + 3 * e].astype(f32)

    sums = layer_one_back(grad, slope1, m1_first, *straight)
    own_grad = jnp.zeros((8, AT), f32)
    drels = []
    for n in range(NB):
        sl = slice(n * AT, (n + 1) * AT)
        b, u = basis_s[:, sl], unit_s[:, sl]
        db, du = first_sums_back(n, sums, b, u, misc_s[1:2, sl])
        drel = drel_s[:, sl] + chain(db, du, slope_s[:, sl], u, misc_s[0:1, sl])
        own_grad = own_grad - drel
        drels.append(drel)
    terms = [t.astype(f32) for t in split3(jnp.concatenate(drels, axis=1))]
    second = far > 0
    terms = [jnp.where(second, 0.0, t) for t in terms] + [
        jnp.where(second, t, 0.0) for t in terms
    ]
    terms = jnp.concatenate(terms, axis=0).astype(bf16)
    copies = []
    for t in (3, 4, 2, 1, 0):
        part = dot(terms, oht[t * AT : (t + 1) * AT, :], NT)
        low = part[:8] + part[8:16] + part[16:24]
        if t == 0:
            total = own_grad + low
            break
        for s, value in zip(TILES[t], (low, part[24:32] + part[32:40] + part[40:48])):
            f_send[s] = value
            copies += halo(
                3,
                lambda h: f_send.at[h, :3],
                lambda h: f_recv.at[h, :3],
                [(s // 3 - 1, s % 3 - 1)],
            )
    pending += copies
    total = total[:3]
    for c in copies:
        c.wait_recv()
    for s in range(9):
        if s != 4:
            total = total + f_recv[s, :3]
    total = total + (2.0 * scale) * long_range
    for p in range(3):
        force_ref[p] = -total[p : p + 1]

    for c in pending:
        c.wait_send()
    for takes, copy in to_owner:
        pl.when(takes)(copy.wait_send)

    @pl.when(owning)
    def _():
        for c in spread:
            c.wait_send()

    for d in range(1, gx_n):
        back(d).wait_send()


def per_device(
    positions,
    species,
    neighbours,
    counts,
    species_embed,
    radial,
    mixing,
    read_hidden,
    read_out,
    charge_map,
    wavevectors,
):
    gx_n, gy_n = lax.axis_size("gx"), lax.axis_size("gy")
    rows = 2 * (charge_map.shape[1] // gx_n)
    vmem = pltpu.VMEM
    sem = pltpu.SemaphoreType.DMA
    scratch = [
        vmem((9, 8, AT), f32),
        vmem((gx_n, 8, AT), f32),
        vmem((9, C, AT), bf16),
        vmem((HALF, E), bf16),
        vmem((NB, 1, AT), jnp.int32),
        vmem((NB, 1, AT), jnp.int32),
        vmem((NB, 2 * C, AT), f32),
        vmem((48, E), f32),
        vmem((2 * C, HALF), bf16),
        vmem((NB, C, AT), bf16),
        vmem((NB, 2 * C, AT), f32),
        vmem((2 * C, E), bf16),
        vmem((8, E), f32),
        vmem((8, E), f32),
        vmem((8, E), f32),
        vmem((8, E), f32),
        vmem((8, E), f32),
        vmem((4, C, AT), f32),
        vmem((gx_n, DEPTH, AT), bf16),
        vmem((gx_n, KZ * rows, AT), f32),
        vmem((KZ * rows, 256), f32),
        vmem((2 * KZ * rows, 128), f32),
        vmem((3 * KZ * rows, DEPTH), bf16),
        vmem((gx_n, rows, AT), f32),
        vmem((gx_n, rows, AT), f32),
        vmem((KZ, rows, LANES), f32),
        vmem((gy_n, rows, LANES), f32),
        vmem((rows, LANES), f32),
        vmem((KZ, rows, LANES), f32),
        vmem((gx_n, 8, AT), f32),
        vmem((gx_n, 8, AT), f32),
        vmem((9, C, AT), bf16),
        vmem((9, C, AT), bf16),
        vmem((9, 8, AT), f32),
        vmem((9, 8, AT), f32),
        sem((4, 9)),
        sem((4, 9)),
        sem((3, gx_n)),
        sem((3, gx_n)),
        sem((gy_n,)),
        sem((gy_n,)),
        sem((gy_n,)),
        sem((KZ,)),
    ]
    arrays = (
        jnp.transpose(positions[0], (1, 0, 2)),
        species,
        jnp.transpose(neighbours[0], (2, 0, 1)),
        counts,
        species_embed,
        radial,
        mixing,
        read_hidden,
        read_out[None],
        charge_map.T,
        wavevectors,
    )
    forces, site_energy = pl.pallas_call(
        functools.partial(kernel, gx_n, gy_n),
        out_shape=(
            jax.ShapeDtypeStruct((3, 1, AT), f32),
            jax.ShapeDtypeStruct((1, 1, AT), f32),
        ),
        in_specs=[pl.BlockSpec(memory_space=pl.ANY)] * len(arrays),
        out_specs=(pl.BlockSpec(memory_space=pltpu.VMEM),) * 2,
        scratch_shapes=[vmem(a.shape, a.dtype) for a in arrays] + [sem((len(arrays),))] + scratch,
        compiler_params=pltpu.CompilerParams(
            collective_id=0, has_side_effects=True, vmem_limit_bytes=60 * 1024 * 1024
        ),
    )(*arrays)
    return jnp.transpose(forces, (1, 0, 2))[None], site_energy


def solution(mesh):
    in_specs = (
        P("gx", "gy", None, None),
        P("gx", "gy", None),
        P("gx", "gy", None, None),
        P("gx", "gy", None),
        P(),
        P(),
        P(),
        P(),
        P(),
        P(),
        P(),
    )
    out_specs = (P("gx", "gy", None, None), P("gx", "gy", None))
    return jax.shard_map(
        per_device, mesh=mesh, in_specs=in_specs, out_specs=out_specs, check_vma=False
    )
```
